256 devices in a mesh: dp: 8 (over y, core), block: 32 (over x, z).
Axes of the slice: x: 4, y: 4, z: 8, core: 2. Of those that a mesh axis runs over, the one named last changes fastest.
Arguments:
- queries: bfloat16 [8, 64, 64, 4096], P('dp', 'block'), may hold values from -24 to 24
- keys_pool: bfloat16 [8, 32, 128, 4096], P('dp', None, None, 'block'), may hold values from -24 to 24
- values_pool: bfloat16 [8, 32, 128, 4096], P('dp', None, None, 'block'), may hold values from -6 to 6
- rel_bias: float32 [32, 192], replicated, may hold values from -4 to 4
- out_grad: bfloat16 [8, 64, 64, 4096], P('dp', 'block'), may hold values from -6 to 6
- fetch_ids: int32 [8, 32, 3], P('dp', 'block'), may hold values from 0 to 31, as said below
- slot_of: int32 [8, 64, 2], P('dp', 'block'), may hold values from 0 to 2, as said below
Outputs:
- attended: bfloat16 [8, 64, 64, 4096], P('dp', 'block')
- query_grad: bfloat16 [8, 64, 64, 4096], P('dp', 'block')
- key_grad: bfloat16 [8, 32, 128, 4096], P('dp', None, None, 'block')
- value_grad: bfloat16 [8, 32, 128, 4096], P('dp', None, None, 'block')
- bias_grad: float32 [32, 192], replicated
The draws below stay inside these ranges and needn't reach their ends.
Inputs may be any that keep to these rules, and one draw needn't show every extreme that they name: `fetch_ids`: A device's fetch list holds 3 different encodings. `slot_of`: every position of a device's fetch list is read by some block of that device; the two neighbours of a block are different, and the first neighbours of a device's blocks are all different.
All inputs are finite; a program needn't handle non-finite values.
Results may differ from the reference program's by a relative error of at most 0.022.
Values may be sent and summed in bfloat16 or wider, within the bound.
No kernel may reach another device: no remote copies, remote signals or barrier semaphores. Data moves between devices by JAX's collectives and lax.ppermute only.
A program may use at most 128 MiB of HBM per device.

```python
import math
import jax
import jax.numpy as jnp
from jax import lax

HEADS = 32
HEAD_DIM = 128
BLOCK = 64
NBLEN = 128
NEIGH = 2
CH_DEV = 2
ENC_DEV = 1
GROUPS = 8
BLOCKS = 64
POOL = 32
CAP = 3
HD = 4096
REL = 192
N_BLOCK = 32


def draw_queries(key, part):
    key = jax.random.fold_in(key, 1)
    key_base = jax.random.fold_in(key, 0)
    full_shape = (GROUPS, BLOCKS, BLOCK, HEADS, HEAD_DIM)
    drawn = jax.random.normal(key_base, full_shape, jnp.float32)
    return jnp.clip(drawn, -24.0, 24.0).reshape(GROUPS, BLOCKS, BLOCK, HD).astype(jnp.bfloat16)


def draw_keys_pool(key, part):
    key = jax.random.fold_in(key, 2)
    key_base = jax.random.fold_in(key, 0)
    full_shape = (GROUPS, POOL, NBLEN, HEADS, HEAD_DIM)
    drawn = jax.random.normal(key_base, full_shape, jnp.float32)
    return jnp.clip(drawn, -24.0, 24.0).reshape(GROUPS, POOL, NBLEN, HD).astype(jnp.bfloat16)


def draw_fetch_ids(key, part):
    key = jax.random.fold_in(key, 11)
    key_shift, key_order, key_score, key_mix = jax.random.split(key, 4)
    multiple = jax.random.randint(key_shift, (GROUPS,), 0, N_BLOCK)
    shift = (ENC_DEV * multiple + ENC_DEV - 1) % POOL
    leading = (jnp.arange(N_BLOCK)[None, :] * ENC_DEV + shift[:, None]) % POOL
    order_scores = jax.random.randint(key_order, (GROUPS, N_BLOCK), 0, 1 << 20) * N_BLOCK + jnp.arange(N_BLOCK)[None, :]
    leading = jnp.take_along_axis(leading, jnp.argsort(order_scores, axis=-1), axis=-1)
    scores = jax.random.randint(key_score, (GROUPS, N_BLOCK, POOL), 0, 1 << 20) * POOL + jnp.arange(POOL)[None, None, :]
    scores = jnp.where(jnp.arange(POOL)[None, None, :] == leading[:, :, None], -1, scores)
    picked = jnp.argsort(scores, axis=-1)[:, :, :CAP]
    mixing = jax.random.randint(key_mix, (GROUPS, N_BLOCK, CAP), 0, 1 << 20) * CAP + jnp.arange(CAP)[None, None, :]
    picked = jnp.take_along_axis(picked, jnp.argsort(mixing, axis=-1), axis=-1)
    return picked.astype(jnp.int32)


def draw_slot_of(key, part):
    key = jax.random.fold_in(key, 3)
    key_order, key_step, key_extra = jax.random.split(key, 3)
    order_scores = jax.random.randint(key_order, (GROUPS, N_BLOCK, CAP), 0, 1 << 20) * CAP + jnp.arange(CAP)[None, None, :]
    orders = jnp.argsort(order_scores, axis=-1).astype(jnp.int32)
    first_slot = orders[:, :, :CH_DEV]
    advance = jax.random.randint(key_step, (GROUPS, N_BLOCK, CH_DEV), 1, CAP)
    partner = (jnp.arange(CH_DEV)[None, None, :] + advance) % CAP
    second_slot = jnp.take_along_axis(orders, partner, axis=-1)
    extra_block = jax.random.randint(key_extra, (GROUPS, N_BLOCK, 1), 0, CH_DEV)
    is_extra = jnp.arange(CH_DEV)[None, None, :] == extra_block
    second_slot = jnp.where(is_extra, orders[:, :, CH_DEV:CH_DEV + 1], second_slot)
    stacked = jnp.stack([first_slot, second_slot], axis=-1)
    return stacked.reshape(GROUPS, BLOCKS, NEIGH).astype(jnp.int32)


def shard_levels(rng, extent, pieces, smallest, largest):
    def one(axis_at, parts):
        heights = jax.random.uniform(jax.random.fold_in(jax.random.fold_in(rng, 6), axis_at), (parts,), jnp.float32, smallest / len(pieces), largest / len(pieces))
        return jnp.repeat(jnp.exp(heights), extent[axis_at] // parts).reshape((-1,) + (1,) * (len(extent) - axis_at - 1))

    factor_of = one(*pieces[0])
    for cut in pieces[1:]:
        factor_of = factor_of * one(*cut)
    return factor_of


def centred(rng, extent, spread, most, cuts=(), kind=jnp.bfloat16):
    level = shard_levels(rng, extent, cuts, -0.22, 0.18) if cuts else 1.0
    values = jax.random.normal(rng, extent, jnp.float32) * spread * level
    return jnp.minimum(jnp.maximum(values, -most), most).astype(kind)


def setup_inputs(seed: int = 0) -> dict:
    key_list = jax.random.split(jax.random.key(seed), 8)
    return {
        "queries": draw_queries(jax.random.fold_in(key_list[7], 71), 0),
        "keys_pool": draw_keys_pool(jax.random.fold_in(key_list[7], 71), 0),
        "values_pool": centred(key_list[2], (GROUPS, POOL, NBLEN, HD), 1.0, 6.0, ((0, 8), (3, 32))),
        "rel_bias": centred(key_list[3], (HEADS, REL), 1.0, 4.0, (), jnp.float32),
        "out_grad": centred(key_list[4], (GROUPS, BLOCKS, BLOCK, HD), 1.0, 6.0, ((0, 8), (1, 32))),
        "fetch_ids": draw_fetch_ids(jax.random.fold_in(key_list[7], 71), 0),
        "slot_of": draw_slot_of(jax.random.fold_in(key_list[7], 71), 0),
    }


def build_bias(rel_bias):
    query_pos = jnp.arange(BLOCK)[:, None]
    key_pos = jnp.arange(NBLEN)[None, :]
    offsets = (key_pos - query_pos + BLOCK - 1).reshape(-1)
    one_hot = (jnp.arange(REL)[:, None] == offsets[None, :]).astype(jnp.float32)
    table = jnp.dot(rel_bias, one_hot, precision=lax.Precision.HIGHEST)
    table = table.reshape(rel_bias.shape[0], BLOCK, NBLEN)
    return (jnp.concatenate([table] * NEIGH, axis=-1), one_hot)

def fold_bias(dscore_sum, one_hot):
    heads_here = dscore_sum.shape[0]
    folded = lax.optimization_barrier(jnp.sum(dscore_sum.reshape(heads_here, BLOCK, NEIGH, NBLEN), axis=2))
    return jnp.dot(folded.reshape(heads_here, BLOCK * NBLEN), one_hot.T, precision=lax.Precision.HIGHEST)

def attention_pass(query_rows, key_rows, value_rows, grad_rows, bias):
    scale = 1.0 / math.sqrt(HEAD_DIM)
    query_wide = query_rows.astype(jnp.float32)
    key_wide = key_rows.astype(jnp.float32)
    value_wide = value_rows.astype(jnp.float32)
    grad_wide = grad_rows.astype(jnp.float32)
    scores = jnp.einsum('cihd,cjhd->chij', query_wide, key_wide) * scale + bias[None]
    top_score = lax.optimization_barrier(jnp.max(scores, axis=-1, keepdims=True))
    expo = jnp.exp(scores - top_score)
    probs = expo / lax.optimization_barrier(jnp.sum(expo, axis=-1, keepdims=True))
    probs_low = probs.astype(jnp.bfloat16).astype(jnp.float32)
    attended = jnp.einsum('chij,cjhd->cihd', probs_low, value_wide).astype(jnp.bfloat16)
    dprobs = jnp.einsum('cihd,cjhd->chij', grad_wide, value_wide)
    inner = lax.optimization_barrier(jnp.sum(probs * dprobs, axis=-1, keepdims=True))
    dscores = probs * (dprobs - inner)
    dscores_low = dscores.astype(jnp.bfloat16).astype(jnp.float32)
    query_grad = (jnp.einsum('chij,cjhd->cihd', dscores_low, key_wide) * scale).astype(jnp.bfloat16)
    key_part = jnp.einsum('chij,cihd->cjhd', dscores_low, query_wide) * scale
    value_part = jnp.einsum('chij,cihd->cjhd', probs_low, grad_wide)
    return (attended, query_grad, key_part, value_part, lax.optimization_barrier(jnp.sum(dscores, axis=0)))

def reference(queries, keys_pool, values_pool, rel_bias, out_grad, fetch_ids, slot_of):
    bias, one_hot = build_bias(rel_bias)
    owner_dev = (jnp.arange(BLOCKS) // CH_DEV).astype(jnp.int32)

    def one_group(inputs):
        group_q, group_k, group_v, group_g, group_fetch, group_slots = inputs
        enc_ids = group_fetch[owner_dev[:, None], group_slots]
        key_rows = group_k[enc_ids].reshape(BLOCKS, NEIGH * NBLEN, HEADS, HEAD_DIM)
        value_rows = group_v[enc_ids].reshape(BLOCKS, NEIGH * NBLEN, HEADS, HEAD_DIM)
        query_rows = group_q.reshape(BLOCKS, BLOCK, HEADS, HEAD_DIM)
        grad_rows = group_g.reshape(BLOCKS, BLOCK, HEADS, HEAD_DIM)
        attended, query_grad, key_part, value_part, dscore_sum = attention_pass(query_rows, key_rows, value_rows, grad_rows, bias)
        flat_ids = enc_ids.reshape(-1)
        key_grad = jax.ops.segment_sum(key_part.reshape(BLOCKS * NEIGH, NBLEN * HD), flat_ids, num_segments=POOL)
        value_grad = jax.ops.segment_sum(value_part.reshape(BLOCKS * NEIGH, NBLEN * HD), flat_ids, num_segments=POOL)
        return (attended.reshape(BLOCKS, BLOCK, HD), query_grad.reshape(BLOCKS, BLOCK, HD), key_grad.astype(jnp.bfloat16).reshape(POOL, NBLEN, HD), value_grad.astype(jnp.bfloat16).reshape(POOL, NBLEN, HD), dscore_sum)
    results = lax.map(one_group, (queries, keys_pool, values_pool, out_grad, fetch_ids, slot_of))
    bias_grad = fold_bias(lax.optimization_barrier(jnp.sum(results[4], axis=0)), one_hot)
    return (results[0], results[1], results[2], results[3], bias_grad)
```

```python
import functools
import math

import jax
import jax.numpy as jnp
from jax import lax
from jax.experimental import pallas as pl
from jax.experimental.pallas import tpu as pltpu
from jax.sharding import PartitionSpec as P

HEADS = 32
HEAD_DIM = 128
BLOCK = 64
NBLEN = 128
NEIGH = 2
CH_DEV = 2
POOL = 32
HD = HEADS * HEAD_DIM
REL = 192
N_BLOCK = 32
N_DP = 8
HALF = CH_DEV * BLOCK
DATA = 2 * HALF
ROWS = DATA + 16
PACK_HEADS = 8
SRC_STEP = 4
SCALE = 1.0 / math.sqrt(HEAD_DIM)

NT = (((1,), (1,)), ((), ()))
TN = (((0,), (0,)), ((), ()))
F32 = jnp.float32
BF16 = jnp.bfloat16


def pack_kernel(fetch_ref, slot_ref, q_ref, g_ref, out_ref):
    lane = lax.broadcasted_iota(jnp.int32, (16, 128), 1)
    ids = jnp.zeros((16, 128), jnp.int32)
    for c in range(CH_DEV):
        for n in range(NEIGH):
            enc = fetch_ref[0, 0, slot_ref[0, c, n]]
            ids = jnp.where(lane == c * NEIGH + n, enc, ids)
    ids = ids.astype(F32).astype(BF16)
    for h in range(PACK_HEADS):
        cols = slice(h * HEAD_DIM, (h + 1) * HEAD_DIM)
        for c in range(CH_DEV):
            out_ref[h, c * BLOCK : (c + 1) * BLOCK] = q_ref[0, c, :, cols]
            out_ref[h, HALF + c * BLOCK : HALF + (c + 1) * BLOCK] = g_ref[0, c, :, cols]
        out_ref[h, DATA:] = ids


def pack(fetch_ids, slot_of, queries, out_grad):
    rows = pl.BlockSpec((1, CH_DEV, BLOCK, PACK_HEADS * HEAD_DIM), lambda i: (0, 0, 0, i))
    return pl.pallas_call(
        pack_kernel,
        grid=(HEADS // PACK_HEADS,),
        in_specs=[
            pl.BlockSpec(memory_space=pltpu.SMEM),
            pl.BlockSpec(memory_space=pltpu.SMEM),
            rows,
            rows,
        ],
        out_specs=pl.BlockSpec((PACK_HEADS, ROWS, HEAD_DIM), lambda i: (i, 0, 0)),
        out_shape=jax.ShapeDtypeStruct((HEADS, ROWS, HEAD_DIM), BF16),
        name="pack_heads",
    )(fetch_ids, slot_of, queries, out_grad)


def attention_kernel(
    head_ref,
    x_ref,
    ids_ref,
    keys_ref,
    values_ref,
    rel_ref,
    y_ref,
    dk_out,
    dv_out,
    bias_out,
    ids_vmem,
    ids_smem,
    bias_ref,
    dsum_ref,
    dk_ref,
    dv_ref,
    sem,
):
    step = pl.program_id(0)
    head = head_ref[0]

    @pl.when(step == 0)
    def _():
        ids_vmem[...] = ids_ref[:, 0, :].astype(F32).astype(jnp.int32)
        copy = pltpu.make_async_copy(ids_vmem, ids_smem, sem)
        copy.start()
        row = rel_ref[pl.ds(head, 1), :]
        wide = jnp.concatenate([row, jnp.zeros((1, 256 - REL), F32)], axis=1)
        wide = jnp.broadcast_to(wide, (BLOCK, 256))
        rolled = pltpu.roll(wide, 256 - (BLOCK - 1), 1, stride=1, stride_axis=0)[:, :NBLEN]
        bias_ref[...] = jnp.concatenate([rolled, rolled], axis=1)
        dsum_ref[...] = jnp.zeros_like(dsum_ref)
        dk_ref[...] = jnp.zeros_like(dk_ref)
        dv_ref[...] = jnp.zeros_like(dv_ref)
        copy.wait()

    def one_source(s, carry):
        src = step * SRC_STEP + s
        dsum = jnp.zeros((BLOCK, NEIGH * NBLEN), F32)
        for c in range(CH_DEV):
            ids = [ids_smem[src, c * NEIGH + n] for n in range(NEIGH)]
            q = x_ref[s, c * BLOCK : (c + 1) * BLOCK]
            g = x_ref[s, HALF + c * BLOCK : HALF + (c + 1) * BLOCK]
            k = jnp.concatenate([keys_ref[0, i] for i in ids], axis=0)
            v = jnp.concatenate([values_ref[0, i] for i in ids], axis=0)
            scores = lax.dot_general(q, k, NT, preferred_element_type=F32)
            scores = scores * SCALE + bias_ref[...]
            dprobs = lax.dot_general(g, v, NT, preferred_element_type=F32)
            expo = jnp.exp(scores - jnp.max(scores, axis=-1, keepdims=True))
            probs = expo * (1.0 / jnp.sum(expo, axis=-1, keepdims=True))
            probs_low = probs.astype(BF16)
            inner = jnp.sum(probs * dprobs, axis=-1, keepdims=True)
            dscores = probs * (dprobs - inner)
            dscores_low = dscores.astype(BF16)
            dsum += dscores
            attended = jnp.dot(probs_low, v, preferred_element_type=F32)
            query_grad = jnp.dot(dscores_low, k, preferred_element_type=F32) * SCALE
            y_ref[s, c * BLOCK : (c + 1) * BLOCK] = attended.astype(BF16)
            y_ref[s, HALF + c * BLOCK : HALF + (c + 1) * BLOCK] = query_grad.astype(BF16)
            dk = lax.dot_general(dscores_low, q, TN, preferred_element_type=F32)
            dv = lax.dot_general(probs_low, g, TN, preferred_element_type=F32)
            for n in range(NEIGH):
                rows = slice(n * NBLEN, (n + 1) * NBLEN)
                dk_ref[ids[n]] += dk[rows]
                dv_ref[ids[n]] += dv[rows]
        dsum_ref[...] += dsum
        return carry

    lax.fori_loop(0, SRC_STEP, one_source, 0, unroll=2)

    @pl.when(step == pl.num_programs(0) - 1)
    def _():
        dk_out[0] = (dk_ref[...] * SCALE).astype(BF16)
        dv_out[0] = dv_ref[...].astype(BF16)
        folded = dsum_ref[:, :NBLEN] + dsum_ref[:, NBLEN:]
        wide = jnp.concatenate([folded, jnp.zeros((BLOCK, NBLEN), F32)], axis=1)
        group = sum(
            pltpu.roll(wide[t : t + 8], BLOCK - 8 - t, 1) if t < BLOCK - 8 else wide[t : t + 8]
            for t in range(0, BLOCK, 8)
        )
        total = sum(
            pltpu.roll(group[r : r + 1], 7 - r, 1) if r < 7 else group[r : r + 1] for r in range(8)
        )[:, :REL]
        here = lax.broadcasted_iota(jnp.int32, (HEADS, REL), 0) == head
        bias_out[...] = jnp.where(here, jnp.broadcast_to(total, (HEADS, REL)), 0.0)


def attention(head, recv, keys_pool, values_pool, rel_bias):
    pool = (1, POOL, NBLEN, HEAD_DIM)
    whole_pool = pl.BlockSpec(pool, lambda i, *_: (0, 0, 0, 0))
    return pl.pallas_call(
        attention_kernel,
        grid_spec=pltpu.PrefetchScalarGridSpec(
            num_scalar_prefetch=1,
            grid=(N_BLOCK // SRC_STEP,),
            in_specs=[
                pl.BlockSpec((SRC_STEP, DATA, HEAD_DIM), lambda i, *_: (i, 0, 0)),
                pl.BlockSpec((N_BLOCK, 16, HEAD_DIM), lambda i, *_: (0, DATA // 16, 0)),
                whole_pool,
                whole_pool,
                pl.BlockSpec((HEADS, REL), lambda i, *_: (0, 0)),
            ],
            out_specs=[
                pl.BlockSpec((SRC_STEP, DATA, HEAD_DIM), lambda i, *_: (i, 0, 0)),
                whole_pool,
                whole_pool,
                pl.BlockSpec((HEADS, REL), lambda i, *_: (0, 0)),
            ],
            scratch_shapes=[
                pltpu.VMEM((N_BLOCK, 128), jnp.int32),
                pltpu.SMEM((N_BLOCK, 128), jnp.int32),
                pltpu.VMEM((BLOCK, NEIGH * NBLEN), F32),
                pltpu.VMEM((BLOCK, NEIGH * NBLEN), F32),
                pltpu.VMEM((POOL, NBLEN, HEAD_DIM), F32),
                pltpu.VMEM((POOL, NBLEN, HEAD_DIM), F32),
                pltpu.SemaphoreType.DMA,
            ],
        ),
        out_shape=[
            jax.ShapeDtypeStruct((N_BLOCK, DATA, HEAD_DIM), BF16),
            jax.ShapeDtypeStruct(pool, BF16),
            jax.ShapeDtypeStruct(pool, BF16),
            jax.ShapeDtypeStruct((HEADS, REL), F32),
        ],
        compiler_params=pltpu.CompilerParams(vmem_limit_bytes=40 * 1024 * 1024),
        name="attention_both",
    )(head, recv, recv, keys_pool, values_pool, rel_bias)


def unpack_kernel(y_ref, att_ref, dq_ref):
    for h in range(PACK_HEADS):
        cols = slice(h * HEAD_DIM, (h + 1) * HEAD_DIM)
        for c in range(CH_DEV):
            att_ref[0, c, :, cols] = y_ref[h, c * BLOCK : (c + 1) * BLOCK]
            dq_ref[0, c, :, cols] = y_ref[h, HALF + c * BLOCK : HALF + (c + 1) * BLOCK]


def unpack(back):
    rows = pl.BlockSpec((1, CH_DEV, BLOCK, PACK_HEADS * HEAD_DIM), lambda i: (0, 0, 0, i))
    shape = jax.ShapeDtypeStruct((1, CH_DEV, BLOCK, HD), BF16)
    return pl.pallas_call(
        unpack_kernel,
        grid=(HEADS // PACK_HEADS,),
        in_specs=[pl.BlockSpec((PACK_HEADS, DATA, HEAD_DIM), lambda i: (i, 0, 0))],
        out_specs=[rows, rows],
        out_shape=[shape, shape],
        name="unpack_heads",
    )(back)


def sum_everywhere(part):
    for axis, size in (("dp", N_DP), ("block", N_BLOCK)):
        hop = 1
        while hop < size:
            part = part + lax.ppermute(part, axis, [(d, d ^ hop) for d in range(size)])
            hop *= 2
    return part


def on_device(queries, keys_pool, values_pool, rel_bias, out_grad, fetch_ids, slot_of):
    head = lax.axis_index("block").astype(jnp.int32).reshape(1)
    sent = pack(fetch_ids, slot_of, queries, out_grad)
    recv = lax.all_to_all(sent, "block", split_axis=0, concat_axis=0, tiled=True)
    y, key_grad, value_grad, bias_part = attention(head, recv, keys_pool, values_pool, rel_bias)
    back = lax.all_to_all(y, "block", split_axis=0, concat_axis=0, tiled=True)
    bias_grad = sum_everywhere(bias_part)
    attended, query_grad = unpack(back)
    return (attended, query_grad, key_grad, value_grad, bias_grad)


def solution(mesh):
    in_specs = (
        P("dp", "block", None, None),
        P("dp", None, None, "block"),
        P("dp", None, None, "block"),
        P(),
        P("dp", "block", None, None),
        P("dp", "block", None),
        P("dp", "block", None),
    )
    out_specs = (
        P("dp", "block", None, None),
        P("dp", "block", None, None),
        P("dp", None, None, "block"),
        P("dp", None, None, "block"),
        P(),
    )
    return jax.shard_map(
        on_device, mesh=mesh, in_specs=in_specs, out_specs=out_specs, check_vma=False
    )
```

```python
import functools
import math

import jax
import jax.numpy as jnp
from jax import lax
from jax.experimental import pallas as pl
from jax.experimental.pallas import tpu as pltpu
from jax.sharding import PartitionSpec as P

HEADS = 32
HEAD_DIM = 128
BLOCK = 64
NBLEN = 128
NEIGH = 2
CH_DEV = 2
POOL = 32
HD = HEADS * HEAD_DIM
REL = 192
N_BLOCK = 32
N_DP = 8
HALF = CH_DEV * BLOCK
DATA = 2 * HALF
ROWS = DATA + 16
PACK_HEADS = 8
SRC_STEP = 4
SCALE = 1.0 / math.sqrt(HEAD_DIM)

NT = (((1,), (1,)), ((), ()))
TN = (((0,), (0,)), ((), ()))
F32 = jnp.float32
BF16 = jnp.bfloat16


def pack_kernel(fetch_ref, slot_ref, q_ref, g_ref, out_ref):
    lane = lax.broadcasted_iota(jnp.int32, (16, 128), 1)
    ids = jnp.zeros((16, 128), jnp.int32)
    for c in range(CH_DEV):
        for n in range(NEIGH):
            enc = fetch_ref[0, 0, slot_ref[0, c, n]]
            ids = jnp.where(lane == c * NEIGH + n, enc, ids)
    ids = ids.astype(F32).astype(BF16)
    for h in range(PACK_HEADS):
        cols = slice(h * HEAD_DIM, (h + 1) * HEAD_DIM)
        for c in range(CH_DEV):
            out_ref[h, c * BLOCK : (c + 1) * BLOCK] = q_ref[0, c, :, cols]
            out_ref[h, HALF + c * BLOCK : HALF + (c + 1) * BLOCK] = g_ref[0, c, :, cols]
        out_ref[h, DATA:] = ids


def pack(fetch_ids, slot_of, queries, out_grad):
    rows = pl.BlockSpec((1, CH_DEV, BLOCK, PACK_HEADS * HEAD_DIM), lambda i: (0, 0, 0, i))
    return pl.pallas_call(
        pack_kernel,
        grid=(HEADS // PACK_HEADS,),
        in_specs=[
            pl.BlockSpec(memory_space=pltpu.SMEM),
            pl.BlockSpec(memory_space=pltpu.SMEM),
            rows,
            rows,
        ],
        out_specs=pl.BlockSpec((PACK_HEADS, ROWS, HEAD_DIM), lambda i: (i, 0, 0)),
        out_shape=jax.ShapeDtypeStruct((HEADS, ROWS, HEAD_DIM), BF16),
        name="pack_heads",
    )(fetch_ids, slot_of, queries, out_grad)


def build_bias(rel_ref, head, bias_ref):
    row = rel_ref[pl.ds(head, 1), :]
    wide = jnp.concatenate([row, jnp.zeros((1, 256 - REL), F32)], axis=1)
    wide = jnp.broadcast_to(wide, (BLOCK, 256))
    rolled = pltpu.roll(wide, 256 - (BLOCK - 1), 1, stride=1, stride_axis=0)[:, :NBLEN]
    bias_ref[...] = jnp.concatenate([rolled, rolled], axis=1)


def fold_bias(dscore_sum):
    folded = dscore_sum[:, :NBLEN] + dscore_sum[:, NBLEN:]
    wide = jnp.concatenate([folded, jnp.zeros((BLOCK, NBLEN), F32)], axis=1)
    group = sum(
        pltpu.roll(wide[t : t + 8], BLOCK - 8 - t, 1) if t < BLOCK - 8 else wide[t : t + 8]
        for t in range(0, BLOCK, 8)
    )
    return sum(
        pltpu.roll(group[r : r + 1], 7 - r, 1) if r < 7 else group[r : r + 1] for r in range(8)
    )


def read_ids(ids_ref, ids_vmem, ids_smem, sem):
    ids_vmem[...] = ids_ref[:, 0, :].astype(F32).astype(jnp.int32)
    copy = pltpu.make_async_copy(ids_vmem, ids_smem, sem)
    copy.start()
    return copy


BLOCKS_STEP = [(s, c) for s in range(SRC_STEP) for c in range(CH_DEV)]


def block_rows(c):
    return slice(c * BLOCK, (c + 1) * BLOCK)


def softmax_parts(step, ids_smem, bias_ref, q_ref, keys_ref, values_ref):
    bias = bias_ref[...]
    ids = [
        [ids_smem[step * SRC_STEP + s, c * NEIGH + n] for n in range(NEIGH)]
        for s, c in BLOCKS_STEP
    ]
    q = [q_ref[s, block_rows(c)] for s, c in BLOCKS_STEP]
    k = [jnp.concatenate([keys_ref[0, i] for i in pair], axis=0) for pair in ids]
    v = [jnp.concatenate([values_ref[0, i] for i in pair], axis=0) for pair in ids]
    scores = [lax.dot_general(a, b, NT, preferred_element_type=F32) for a, b in zip(q, k)]
    scores = [a * SCALE + bias for a in scores]
    tops = [jnp.max(a, axis=-1, keepdims=True) for a in scores]
    expo = [jnp.exp(a - b) for a, b in zip(scores, tops)]
    inverse = [1.0 / jnp.sum(a, axis=-1, keepdims=True) for a in expo]
    probs = [a * b for a, b in zip(expo, inverse)]
    return ids, q, k, v, probs


def forward_kernel(
    head_ref, q_ref, ids_ref, keys_ref, values_ref, rel_ref, y_ref, ids_vmem, ids_smem, bias_ref, sem
):
    step = pl.program_id(0)

    @pl.when(step == 0)
    def _():
        copy = read_ids(ids_ref, ids_vmem, ids_smem, sem)
        build_bias(rel_ref, head_ref[0], bias_ref)
        copy.wait()

    ids, q, k, v, probs = softmax_parts(step, ids_smem, bias_ref, q_ref, keys_ref, values_ref)
    for i, (s, c) in enumerate(BLOCKS_STEP):
        attended = jnp.dot(probs[i].astype(BF16), v[i], preferred_element_type=F32)
        y_ref[s, block_rows(c)] = attended.astype(BF16)


def backward_kernel(
    head_ref,
    q_ref,
    g_ref,
    ids_ref,
    keys_ref,
    values_ref,
    rel_ref,
    y_ref,
    dk_out,
    dv_out,
    bias_out,
    ids_vmem,
    ids_smem,
    bias_ref,
    dsum_ref,
    dk_ref,
    dv_ref,
    sem,
):
    step = pl.program_id(0)

    @pl.when(step == 0)
    def _():
        copy = read_ids(ids_ref, ids_vmem, ids_smem, sem)
        build_bias(rel_ref, head_ref[0], bias_ref)
        dsum_ref[...] = jnp.zeros_like(dsum_ref)
        dk_ref[...] = jnp.zeros_like(dk_ref)
        dv_ref[...] = jnp.zeros_like(dv_ref)
        copy.wait()

    ids, q, k, v, probs = softmax_parts(step, ids_smem, bias_ref, q_ref, keys_ref, values_ref)
    g = [g_ref[s, block_rows(c)] for s, c in BLOCKS_STEP]
    dprobs = [lax.dot_general(a, b, NT, preferred_element_type=F32) for a, b in zip(g, v)]
    probs_low = [a.astype(BF16) for a in probs]
    inner = [jnp.sum(a * b, axis=-1, keepdims=True) for a, b in zip(probs, dprobs)]
    dscores = [a * (b - c) for a, b, c in zip(probs, dprobs, inner)]
    dscores_low = [a.astype(BF16) for a in dscores]
    dsum_ref[...] += sum(dscores)
    for i, (s, c) in enumerate(BLOCKS_STEP):
        query_grad = jnp.dot(dscores_low[i], k[i], preferred_element_type=F32) * SCALE
        y_ref[s, block_rows(c)] = query_grad.astype(BF16)
    dk = [lax.dot_general(a, b, TN, preferred_element_type=F32) for a, b in zip(dscores_low, q)]
    dv = [lax.dot_general(a, b, TN, preferred_element_type=F32) for a, b in zip(probs_low, g)]
    for i in range(len(BLOCKS_STEP)):
        for n in range(NEIGH):
            rows = slice(n * NBLEN, (n + 1) * NBLEN)
            dk_ref[ids[i][n]] += dk[i][rows]
            dv_ref[ids[i][n]] += dv[i][rows]

    @pl.when(step == pl.num_programs(0) - 1)
    def _():
        dk_out[0] = (dk_ref[...] * SCALE).astype(BF16)
        dv_out[0] = dv_ref[...].astype(BF16)
        bias_out[...] = fold_bias(dsum_ref[...])


POOL_SHAPE = (1, POOL, NBLEN, HEAD_DIM)
POOL_SPEC = pl.BlockSpec(POOL_SHAPE, lambda i, *_: (0, 0, 0, 0))
REL_SPEC = pl.BlockSpec((HEADS, REL), lambda i, *_: (0, 0))
IDS_SPEC = pl.BlockSpec((N_BLOCK, 16, HEAD_DIM), lambda i, *_: (0, DATA // 16, 0))
Q_SPEC = pl.BlockSpec((SRC_STEP, HALF, HEAD_DIM), lambda i, *_: (i, 0, 0))
G_SPEC = pl.BlockSpec((SRC_STEP, HALF, HEAD_DIM), lambda i, *_: (i, 1, 0))
BIAS_SHAPE = (BLOCK, NEIGH * NBLEN)
IDS_SCRATCH = [pltpu.VMEM((N_BLOCK, 128), jnp.int32), pltpu.SMEM((N_BLOCK, 128), jnp.int32)]


def forward(head, recv, keys_pool, values_pool, rel_bias):
    return pl.pallas_call(
        forward_kernel,
        grid_spec=pltpu.PrefetchScalarGridSpec(
            num_scalar_prefetch=1,
            grid=(N_BLOCK // SRC_STEP,),
            in_specs=[Q_SPEC, IDS_SPEC, POOL_SPEC, POOL_SPEC, REL_SPEC],
            out_specs=Q_SPEC,
            scratch_shapes=[*IDS_SCRATCH, pltpu.VMEM(BIAS_SHAPE, F32), pltpu.SemaphoreType.DMA],
        ),
        out_shape=jax.ShapeDtypeStruct((N_BLOCK, HALF, HEAD_DIM), BF16),
        compiler_params=pltpu.CompilerParams(vmem_limit_bytes=24 * 1024 * 1024),
        cost_estimate=pl.CostEstimate(flops=10**9, bytes_accessed=4 * 10**6, transcendentals=10**6),
        name="attention_forward",
    )(head, recv, recv, keys_pool, values_pool, rel_bias)


def backward(head, recv, keys_pool, values_pool, rel_bias):
    return pl.pallas_call(
        backward_kernel,
        grid_spec=pltpu.PrefetchScalarGridSpec(
            num_scalar_prefetch=1,
            grid=(N_BLOCK // SRC_STEP,),
            in_specs=[Q_SPEC, G_SPEC, IDS_SPEC, POOL_SPEC, POOL_SPEC, REL_SPEC],
            out_specs=[
                Q_SPEC,
                POOL_SPEC,
                POOL_SPEC,
                pl.BlockSpec((1, 256), lambda i, *_: (0, 0)),
            ],
            scratch_shapes=[
                *IDS_SCRATCH,
                pltpu.VMEM(BIAS_SHAPE, F32),
                pltpu.VMEM(BIAS_SHAPE, F32),
                pltpu.VMEM((POOL, NBLEN, HEAD_DIM), F32),
                pltpu.VMEM((POOL, NBLEN, HEAD_DIM), F32),
                pltpu.SemaphoreType.DMA,
            ],
        ),
        out_shape=[
            jax.ShapeDtypeStruct((N_BLOCK, HALF + 16, HEAD_DIM), BF16),
            jax.ShapeDtypeStruct(POOL_SHAPE, BF16),
            jax.ShapeDtypeStruct(POOL_SHAPE, BF16),
            jax.ShapeDtypeStruct((1, 256), F32),
        ],
        compiler_params=pltpu.CompilerParams(vmem_limit_bytes=36 * 1024 * 1024),
        cost_estimate=pl.CostEstimate(flops=3 * 10**9, bytes_accessed=9 * 10**6, transcendentals=10**6),
        name="attention_backward",
    )(head, recv, recv, recv, keys_pool, values_pool, rel_bias)


def add_row_kernel(row_ref, _, y_ref):
    row = row_ref[...]
    high = row.astype(BF16)
    rest = row - high.astype(F32)
    middle = rest.astype(BF16)
    low = (rest - middle.astype(F32)).astype(BF16)
    lines = [part.astype(F32)[:, c : c + 128] for part in (high, middle, low) for c in (0, 128)]
    block = jnp.concatenate([*lines, jnp.zeros((10, 128), F32)], axis=0).astype(BF16)
    y_ref[...] = jnp.broadcast_to(block[None], y_ref.shape)


def add_row(row, y):
    return pl.pallas_call(
        add_row_kernel,
        grid=(1,),
        in_specs=[
            pl.BlockSpec((1, 256), lambda i: (0, 0)),
            pl.BlockSpec(memory_space=pl.ANY),
        ],
        out_specs=pl.BlockSpec((N_BLOCK, 16, HEAD_DIM), lambda i: (0, HALF // 16, 0)),
        out_shape=jax.ShapeDtypeStruct(y.shape, BF16),
        input_output_aliases={1: 0},
        name="add_bias_row",
    )(row, y)


def unpack_kernel(y_ref, out_ref):
    for h in range(PACK_HEADS):
        cols = slice(h * HEAD_DIM, (h + 1) * HEAD_DIM)
        for c in range(CH_DEV):
            out_ref[0, c, :, cols] = y_ref[h, block_rows(c)]


def unpack_bias_kernel(y_ref, out_ref, bias_ref):
    unpack_kernel(y_ref, out_ref)
    lines = y_ref[:, HALF:, :].astype(F32)
    part = [lines[:, r, :] for r in range(6)]
    left = (part[0] + part[2]) + part[4]
    right = (part[1] + part[3]) + part[5]
    bias_ref[...] = jnp.concatenate([left, right], axis=1)[:, :REL]


def unpack(back):
    rows = pl.BlockSpec((1, CH_DEV, BLOCK, PACK_HEADS * HEAD_DIM), lambda i: (0, 0, 0, i))
    shape = jax.ShapeDtypeStruct((1, CH_DEV, BLOCK, HD), BF16)
    with_bias = back.shape[1] > HALF
    out = pl.pallas_call(
        unpack_bias_kernel if with_bias else unpack_kernel,
        grid=(HEADS // PACK_HEADS,),
        in_specs=[pl.BlockSpec((PACK_HEADS, back.shape[1], HEAD_DIM), lambda i: (i, 0, 0))],
        out_specs=[rows] + [pl.BlockSpec((PACK_HEADS, REL), lambda i: (i, 0))] * with_bias,
        out_shape=[shape] + [jax.ShapeDtypeStruct((HEADS, REL), F32)] * with_bias,
        name="unpack_heads",
    )(back)
    return out


def sum_groups(part):
    for hop in (1, 2, 4):
        part = part + lax.ppermute(part, "dp", [(d, d ^ hop) for d in range(N_DP)])
    return part


def all_to_all(parts):
    return lax.all_to_all(parts, "block", split_axis=0, concat_axis=0, tiled=True)


def on_device(queries, keys_pool, values_pool, rel_bias, out_grad, fetch_ids, slot_of):
    head = lax.axis_index("block").astype(jnp.int32).reshape(1)
    recv = all_to_all(pack(fetch_ids, slot_of, queries, out_grad))
    y = forward(head, recv, keys_pool, values_pool, rel_bias)
    back_y = all_to_all(y)
    recv, _ = lax.optimization_barrier((recv, y))
    dq, key_grad, value_grad, bias_part = backward(head, recv, keys_pool, values_pool, rel_bias)
    back_dq = all_to_all(add_row(sum_groups(bias_part), dq))
    (attended,) = unpack(back_y)
    query_grad, bias_grad = unpack(back_dq)
    return (attended, query_grad, key_grad, value_grad, bias_grad)


def solution(mesh):
    in_specs = (
        P("dp", "block", None, None),
        P("dp", None, None, "block"),
        P("dp", None, None, "block"),
        P(),
        P("dp", "block", None, None),
        P("dp", "block", None),
        P("dp", "block", None),
    )
    out_specs = (
        P("dp", "block", None, None),
        P("dp", "block", None, None),
        P("dp", None, None, "block"),
        P("dp", None, None, "block"),
        P(),
    )
    return jax.shard_map(
        on_device, mesh=mesh, in_specs=in_specs, out_specs=out_specs, check_vma=False
    )
```

```python
import functools
import math

import jax
import jax.numpy as jnp
from jax import lax
from jax.experimental import pallas as pl
from jax.experimental.pallas import tpu as pltpu
from jax.sharding import PartitionSpec as P

HEADS = 32
HEAD_DIM = 128
BLOCK = 64
NBLEN = 128
NEIGH = 2
CH_DEV = 2
POOL = 32
HD = HEADS * HEAD_DIM
REL = 192
N_BLOCK = 32
N_DP = 8
X_SIZE = 4
Z_SIZE = 8
HALF = CH_DEV * BLOCK
EXTRA = 8
PACK_HEADS = 8
SRC_STEP = 4
SCALE = 1.0 / math.sqrt(HEAD_DIM)

NT = (((1,), (1,)), ((), ()))
TN = (((0,), (0,)), ((), ()))
F32 = jnp.float32
BF16 = jnp.bfloat16


VMEM_SPEC = pl.BlockSpec(memory_space=pltpu.VMEM)
SMEM_SPEC = pl.BlockSpec(memory_space=pltpu.SMEM)
ANY_SPEC = pl.BlockSpec(memory_space=pl.ANY)
HBM_SPEC = pl.BlockSpec(memory_space=pltpu.HBM)
CHUNKS = HEADS // PACK_HEADS
CHUNK_WIDTH = PACK_HEADS * HEAD_DIM


def block_rows(c):
    return slice(c * BLOCK, (c + 1) * BLOCK)


def head_columns(h):
    return slice(h * HEAD_DIM, (h + 1) * HEAD_DIM)


def vmem_limit(mib):
    return pltpu.CompilerParams(vmem_limit_bytes=mib * 1024 * 1024)


def start(source, target, sem):
    copy = pltpu.make_async_copy(source, target, sem)
    copy.start()
    return copy


def pack_queries_kernel(fetch_ref, slot_ref, q_ref, out_ref, q_buf, out_buf, in_sems, out_sems):
    copies = []
    for i in range(CHUNKS):
        cols = slice(i * CHUNK_WIDTH, (i + 1) * CHUNK_WIDTH)
        copies.append(start(q_ref.at[0, :, :, cols], q_buf.at[:, :, cols], in_sems.at[i]))
    lane = lax.broadcasted_iota(jnp.int32, (EXTRA, 128), 1)
    ids = jnp.zeros((EXTRA, 128), jnp.int32)
    for c in range(CH_DEV):
        for n in range(NEIGH):
            enc = fetch_ref[0, 0, slot_ref[0, c, n]]
            ids = jnp.where(lane == c * NEIGH + n, enc, ids)
    ids = ids.astype(F32).astype(BF16)
    outs = []
    for i in range(CHUNKS):
        heads = slice(i * PACK_HEADS, (i + 1) * PACK_HEADS)
        copies[i].wait()
        for h in range(i * PACK_HEADS, (i + 1) * PACK_HEADS):
            for c in range(CH_DEV):
                out_buf[h, block_rows(c)] = q_buf[c, :, head_columns(h)]
            out_buf[h, HALF:] = ids
        outs.append(start(out_buf.at[heads], out_ref.at[heads], out_sems.at[i]))
    for copy in outs:
        copy.wait()


def pack_queries(fetch_ids, slot_of, queries):
    return pl.pallas_call(
        pack_queries_kernel,
        in_specs=[SMEM_SPEC, SMEM_SPEC, ANY_SPEC],
        out_specs=ANY_SPEC,
        out_shape=jax.ShapeDtypeStruct((HEADS, HALF + EXTRA, HEAD_DIM), BF16),
        scratch_shapes=[
            pltpu.VMEM((CH_DEV, BLOCK, HD), BF16),
            pltpu.VMEM((HEADS, HALF + EXTRA, HEAD_DIM), BF16),
            pltpu.SemaphoreType.DMA((CHUNKS,)),
            pltpu.SemaphoreType.DMA((CHUNKS,)),
        ],
        compiler_params=vmem_limit(60),
        cost_estimate=pl.CostEstimate(flops=10**11, bytes_accessed=2 * 10**6, transcendentals=0),
        name="pack_queries",
    )(fetch_ids, slot_of, queries)


def pack_grads_kernel(head_ref, g_ref, *refs):
    out_refs, (g_buf, out_buf, in_sems, out_sems) = refs[:X_SIZE], refs[X_SIZE:]
    copies = []
    for i in range(X_SIZE):
        column = lax.rem(head_ref[0] // Z_SIZE + i, X_SIZE) * CHUNK_WIDTH
        cols = pl.ds(pl.multiple_of(column, CHUNK_WIDTH), CHUNK_WIDTH)
        copies.append(start(g_ref.at[0, :, :, cols], g_buf.at[i], in_sems.at[i]))
    outs = []
    for i in range(X_SIZE):
        copies[i].wait()
        for h in range(Z_SIZE):
            for c in range(CH_DEV):
                out_buf[i, h, block_rows(c)] = g_buf[i, c, :, head_columns(h)]
        outs.append(start(out_buf.at[i], out_refs[i], out_sems.at[i]))
    for copy in outs:
        copy.wait()


def pack_grads(head, out_grad):
    shape = (Z_SIZE, HALF, HEAD_DIM)
    return pl.pallas_call(
        pack_grads_kernel,
        in_specs=[SMEM_SPEC, ANY_SPEC],
        out_specs=[ANY_SPEC] * X_SIZE,
        out_shape=[jax.ShapeDtypeStruct(shape, BF16)] * X_SIZE,
        scratch_shapes=[
            pltpu.VMEM((X_SIZE, CH_DEV, BLOCK, CHUNK_WIDTH), BF16),
            pltpu.VMEM((X_SIZE, *shape), BF16),
            pltpu.SemaphoreType.DMA((X_SIZE,)),
            pltpu.SemaphoreType.DMA((X_SIZE,)),
        ],
        compiler_params=vmem_limit(60),
        cost_estimate=pl.CostEstimate(flops=0, bytes_accessed=2 * 10**6, transcendentals=0),
        name="pack_grads",
    )(head, out_grad)


def regroup_kernel(head_ref, *refs):
    in_refs, out_refs = refs[:X_SIZE], refs[X_SIZE : X_SIZE + Z_SIZE]
    buf, in_sems, out_sems = refs[X_SIZE + Z_SIZE :]
    copies = [start(in_refs[i], buf.at[i], in_sems.at[i]) for i in range(X_SIZE)]
    for copy in copies:
        copy.wait()
    copies = []
    for k in range(Z_SIZE):
        owner = lax.rem(head_ref[0] + k, Z_SIZE)
        copies.append(start(buf.at[:, owner], out_refs[k], out_sems.at[k]))
    for copy in copies:
        copy.wait()


def regroup(head, parts):
    return pl.pallas_call(
        regroup_kernel,
        in_specs=[SMEM_SPEC] + [ANY_SPEC] * X_SIZE,
        out_specs=[ANY_SPEC] * Z_SIZE,
        out_shape=[jax.ShapeDtypeStruct((X_SIZE, HALF, HEAD_DIM), BF16)] * Z_SIZE,
        scratch_shapes=[
            pltpu.VMEM((X_SIZE, Z_SIZE, HALF, HEAD_DIM), BF16),
            pltpu.SemaphoreType.DMA((X_SIZE,)),
            pltpu.SemaphoreType.DMA((Z_SIZE,)),
        ],
        compiler_params=vmem_limit(60),
        cost_estimate=pl.CostEstimate(flops=10**11, bytes_accessed=2 * 10**6, transcendentals=0),
        name="regroup_grads",
    )(head, *parts)


def send_by(part, dx, dz):
    pairs = [
        (x * Z_SIZE + z, (x + dx) % X_SIZE * Z_SIZE + (z + dz) % Z_SIZE)
        for x in range(X_SIZE)
        for z in range(Z_SIZE)
    ]
    return lax.ppermute(part, "block", pairs)


def build_bias(rel_ref, head, bias_ref):
    row = rel_ref[pl.ds(head, 1), :]
    wide = jnp.concatenate([row, jnp.zeros((1, 256 - REL), F32)], axis=1)
    wide = jnp.broadcast_to(wide, (BLOCK, 256))
    rolled = pltpu.roll(wide, 256 - (BLOCK - 1), 1, stride=1, stride_axis=0)[:, :NBLEN]
    bias_ref[...] = jnp.concatenate([rolled, rolled], axis=1)


def fold_bias(dscore_sum):
    folded = dscore_sum[:, :NBLEN] + dscore_sum[:, NBLEN:]
    wide = jnp.concatenate([folded, jnp.zeros((BLOCK, NBLEN), F32)], axis=1)
    group = sum(
        pltpu.roll(wide[t : t + 8], BLOCK - 8 - t, 1) if t < BLOCK - 8 else wide[t : t + 8]
        for t in range(0, BLOCK, 8)
    )
    return sum(
        pltpu.roll(group[r : r + 1], 7 - r, 1) if r < 7 else group[r : r + 1] for r in range(8)
    )


def read_ids(x_ref, ids_vmem, ids_smem, sem):
    ids_vmem[...] = x_ref[:, HALF, :].astype(F32).astype(jnp.int32)
    copy = pltpu.make_async_copy(ids_vmem, ids_smem, sem)
    copy.start()
    return copy


BLOCKS_STEP = [(s, c) for s in range(SRC_STEP) for c in range(CH_DEV)]


def softmax_parts(sources, ids_smem, bias_ref, x_ref, keys_ref, values_ref):
    bias = bias_ref[...]
    ids = [[ids_smem[sources[s], c * NEIGH + n] for n in range(NEIGH)] for s, c in BLOCKS_STEP]
    q = [x_ref[sources[s], block_rows(c)] for s, c in BLOCKS_STEP]
    k = [jnp.concatenate([keys_ref[0, i] for i in pair], axis=0) for pair in ids]
    v = [jnp.concatenate([values_ref[0, i] for i in pair], axis=0) for pair in ids]
    scores = [lax.dot_general(a, b, NT, preferred_element_type=F32) for a, b in zip(q, k)]
    scores = [a * SCALE + bias for a in scores]
    tops = [jnp.max(a, axis=-1, keepdims=True) for a in scores]
    expo = [jnp.exp(a - b) for a, b in zip(scores, tops)]
    inverse = [1.0 / jnp.sum(a, axis=-1, keepdims=True) for a in expo]
    probs = [a * b for a, b in zip(expo, inverse)]
    return ids, q, k, v, probs


def forward_kernel(
    head_ref, x_ref, keys_ref, values_ref, rel_ref, y_ref, ids_vmem, ids_smem, bias_ref, sem
):
    copy = read_ids(x_ref, ids_vmem, ids_smem, sem)
    build_bias(rel_ref, head_ref[0], bias_ref)
    copy.wait()

    def step(t, carry):
        sources = [t * SRC_STEP + s for s in range(SRC_STEP)]
        ids, q, k, v, probs = softmax_parts(
            sources, ids_smem, bias_ref, x_ref, keys_ref, values_ref
        )
        for i, (s, c) in enumerate(BLOCKS_STEP):
            attended = jnp.dot(probs[i].astype(BF16), v[i], preferred_element_type=F32)
            y_ref[sources[s], block_rows(c)] = attended.astype(BF16)
        return carry

    lax.fori_loop(0, N_BLOCK // SRC_STEP, step, 0)


def near_sources(index, t):
    x, z = index // Z_SIZE, lax.rem(index, Z_SIZE)
    z_source = lax.rem(z + Z_SIZE - t, Z_SIZE)
    return [lax.rem(x + X_SIZE - s, X_SIZE) * Z_SIZE + z_source for s in range(SRC_STEP)]


def score_grads(sources, t, ids_smem, bias_ref, x_ref, g_buf, keys_ref, values_ref):
    ids, q, k, v, probs = softmax_parts(
        sources, ids_smem, bias_ref, x_ref, keys_ref, values_ref
    )
    g = [g_buf[t, s, block_rows(c)] for s, c in BLOCKS_STEP]
    dprobs = [lax.dot_general(a, b, NT, preferred_element_type=F32) for a, b in zip(g, v)]
    inner = [jnp.sum(a * b, axis=-1, keepdims=True) for a, b in zip(probs, dprobs)]
    dscores = [a * (b - c) for a, b, c in zip(probs, dprobs, inner)]
    return ids, q, k, g, probs, dscores


def query_grad_kernel(head_ref, x_ref, keys_ref, values_ref, rel_ref, *refs):
    g_refs = refs[:Z_SIZE]
    y_ref, bias_out, ids_vmem, ids_smem, bias_ref, dsum_ref, g_buf, sem, g_sems = refs[Z_SIZE:]
    g_copies = [start(g_refs[k], g_buf.at[k], g_sems.at[k]) for k in range(Z_SIZE)]
    copy = read_ids(x_ref, ids_vmem, ids_smem, sem)
    build_bias(rel_ref, head_ref[0], bias_ref)
    dsum_ref[...] = jnp.zeros_like(dsum_ref)
    copy.wait()
    for g_copy in g_copies:
        g_copy.wait()

    def step(t, carry):
        sources = near_sources(head_ref[0], t)
        _, _, k, _, _, dscores = score_grads(
            sources, t, ids_smem, bias_ref, x_ref, g_buf, keys_ref, values_ref
        )
        dsum_ref[...] += sum(dscores)
        for i, (s, c) in enumerate(BLOCKS_STEP):
            low = dscores[i].astype(BF16)
            query_grad = jnp.dot(low, k[i], preferred_element_type=F32) * SCALE
            y_ref[sources[s], block_rows(c)] = query_grad.astype(BF16)
        return carry

    lax.fori_loop(0, Z_SIZE, step, 0)
    bias_out[...] = fold_bias(dsum_ref[...])


def pool_grad_kernel(head_ref, x_ref, keys_ref, values_ref, rel_ref, *refs):
    g_refs = refs[:Z_SIZE]
    dk_out, dv_out, ids_vmem, ids_smem, bias_ref, dk_ref, dv_ref, g_buf, sem, g_sems = refs[Z_SIZE:]
    g_copies = [start(g_refs[k], g_buf.at[k], g_sems.at[k]) for k in range(Z_SIZE)]
    copy = read_ids(x_ref, ids_vmem, ids_smem, sem)
    build_bias(rel_ref, head_ref[0], bias_ref)
    dk_ref[...] = jnp.zeros_like(dk_ref)
    dv_ref[...] = jnp.zeros_like(dv_ref)
    copy.wait()
    for g_copy in g_copies:
        g_copy.wait()

    def step(t, carry):
        sources = near_sources(head_ref[0], t)
        ids, q, _, g, probs, dscores = score_grads(
            sources, t, ids_smem, bias_ref, x_ref, g_buf, keys_ref, values_ref
        )
        dscores_low = [a.astype(BF16) for a in dscores]
        probs_low = [a.astype(BF16) for a in probs]
        dk = [lax.dot_general(a, b, TN, preferred_element_type=F32) for a, b in zip(dscores_low, q)]
        dv = [lax.dot_general(a, b, TN, preferred_element_type=F32) for a, b in zip(probs_low, g)]
        for i in range(len(BLOCKS_STEP)):
            for n in range(NEIGH):
                rows = slice(n * NBLEN, (n + 1) * NBLEN)
                dk_ref[ids[i][n]] += dk[i][rows]
                dv_ref[ids[i][n]] += dv[i][rows]
        return carry

    lax.fori_loop(0, Z_SIZE, step, 0)
    dk_out[0] = (dk_ref[...] * SCALE).astype(BF16)
    dv_out[0] = dv_ref[...].astype(BF16)


POOL_SHAPE = (1, POOL, NBLEN, HEAD_DIM)
BIAS_SHAPE = (BLOCK, NEIGH * NBLEN)
IDS_SCRATCH = [pltpu.VMEM((N_BLOCK, 128), jnp.int32), pltpu.SMEM((N_BLOCK, 128), jnp.int32)]


def forward(head, recv, keys_pool, values_pool, rel_bias):
    return pl.pallas_call(
        forward_kernel,
        in_specs=[SMEM_SPEC] + [VMEM_SPEC] * 4,
        out_specs=VMEM_SPEC,
        out_shape=jax.ShapeDtypeStruct((N_BLOCK, HALF, HEAD_DIM), BF16),
        scratch_shapes=[*IDS_SCRATCH, pltpu.VMEM(BIAS_SHAPE, F32), pltpu.SemaphoreType.DMA],
        compiler_params=vmem_limit(16),
        cost_estimate=pl.CostEstimate(flops=10**11, bytes_accessed=4 * 10**6, transcendentals=10**6),
        name="attention_forward",
    )(head, recv, keys_pool, values_pool, rel_bias)


def query_grads(head, recv, grads, keys_pool, values_pool, rel_bias):
    return pl.pallas_call(
        query_grad_kernel,
        in_specs=[SMEM_SPEC] + [VMEM_SPEC] * 4 + [ANY_SPEC] * Z_SIZE,
        out_specs=[VMEM_SPEC] * 2,
        out_shape=[
            jax.ShapeDtypeStruct((N_BLOCK, HALF + EXTRA, HEAD_DIM), BF16),
            jax.ShapeDtypeStruct((1, 256), F32),
        ],
        scratch_shapes=[
            *IDS_SCRATCH,
            pltpu.VMEM(BIAS_SHAPE, F32),
            pltpu.VMEM(BIAS_SHAPE, F32),
            pltpu.VMEM((Z_SIZE, X_SIZE, HALF, HEAD_DIM), BF16),
            pltpu.SemaphoreType.DMA,
            pltpu.SemaphoreType.DMA((Z_SIZE,)),
        ],
        compiler_params=vmem_limit(16),
        cost_estimate=pl.CostEstimate(flops=10**11, bytes_accessed=5 * 10**6, transcendentals=10**6),
        name="query_grads",
    )(head, recv, keys_pool, values_pool, rel_bias, *grads)


def pool_grads(head, recv, grads, keys_pool, values_pool, rel_bias):
    return pl.pallas_call(
        pool_grad_kernel,
        in_specs=[SMEM_SPEC] + [VMEM_SPEC] * 4 + [ANY_SPEC] * Z_SIZE,
        out_specs=[VMEM_SPEC] * 2,
        out_shape=[jax.ShapeDtypeStruct(POOL_SHAPE, BF16)] * 2,
        scratch_shapes=[
            *IDS_SCRATCH,
            pltpu.VMEM(BIAS_SHAPE, F32),
            pltpu.VMEM(POOL_SHAPE[1:], F32),
            pltpu.VMEM(POOL_SHAPE[1:], F32),
            pltpu.VMEM((Z_SIZE, X_SIZE, HALF, HEAD_DIM), BF16),
            pltpu.SemaphoreType.DMA,
            pltpu.SemaphoreType.DMA((Z_SIZE,)),
        ],
        compiler_params=vmem_limit(24),
        cost_estimate=pl.CostEstimate(flops=10**11, bytes_accessed=6 * 10**6, transcendentals=10**6),
        name="pool_grads",
    )(head, recv, keys_pool, values_pool, rel_bias, *grads)


def add_row_kernel(row_ref, _, y_ref, block_ref, sem):
    row = row_ref[...]
    high = row.astype(BF16)
    rest = row - high.astype(F32)
    middle = rest.astype(BF16)
    low = (rest - middle.astype(F32)).astype(BF16)
    lines = [part.astype(F32)[:, c : c + 128] for part in (high, middle, low) for c in (0, 128)]
    block = jnp.concatenate([*lines, jnp.zeros((EXTRA - 6, 128), F32)], axis=0).astype(BF16)
    block_ref[...] = jnp.broadcast_to(block[None], block_ref.shape)
    copy = pltpu.make_async_copy(block_ref, y_ref.at[:, HALF:], sem)
    copy.start()
    copy.wait()


def add_row(row, y):
    return pl.pallas_call(
        add_row_kernel,
        in_specs=[VMEM_SPEC, ANY_SPEC],
        out_specs=ANY_SPEC,
        out_shape=jax.ShapeDtypeStruct(y.shape, BF16),
        scratch_shapes=[pltpu.VMEM((N_BLOCK, EXTRA, HEAD_DIM), BF16), pltpu.SemaphoreType.DMA],
        input_output_aliases={1: 0},
        compiler_params=vmem_limit(4),
        name="add_bias_row",
    )(row, y)


def unpack_kernel(y_ref, out_ref, buf, sems):
    copies = []
    for i in range(CHUNKS):
        for h in range(i * PACK_HEADS, (i + 1) * PACK_HEADS):
            for c in range(CH_DEV):
                buf[c, :, head_columns(h)] = y_ref[h, block_rows(c)]
        cols = slice(i * CHUNK_WIDTH, (i + 1) * CHUNK_WIDTH)
        copy = pltpu.make_async_copy(buf.at[:, :, cols], out_ref.at[0, :, :, cols], sems.at[i])
        copy.start()
        copies.append(copy)
    for copy in copies:
        copy.wait()


def unpack_bias_kernel(y_ref, out_ref, bias_ref, buf, sems):
    lines = y_ref[:, HALF:, :].astype(F32)
    part = [lines[:, r, :] for r in range(6)]
    left = (part[0] + part[2]) + part[4]
    right = (part[1] + part[3]) + part[5]
    bias_ref[...] = jnp.concatenate([left, right], axis=1)[:, :REL]
    unpack_kernel(y_ref, out_ref, buf, sems)


def unpack(back):
    shape = jax.ShapeDtypeStruct((1, CH_DEV, BLOCK, HD), BF16)
    with_bias = back.shape[1] > HALF
    return pl.pallas_call(
        unpack_bias_kernel if with_bias else unpack_kernel,
        in_specs=[VMEM_SPEC],
        out_specs=[HBM_SPEC] + [VMEM_SPEC] * with_bias,
        out_shape=[shape] + [jax.ShapeDtypeStruct((HEADS, REL), F32)] * with_bias,
        scratch_shapes=[pltpu.VMEM((CH_DEV, BLOCK, HD), BF16), pltpu.SemaphoreType.DMA((CHUNKS,))],
        compiler_params=vmem_limit(8),
        name="unpack_heads",
    )(back)


def sum_groups(part):
    for hop in (1, 2, 4):
        part = part + lax.ppermute(part, "dp", [(d, d ^ hop) for d in range(N_DP)])
    return part


def all_to_all(parts):
    return lax.all_to_all(parts, "block", split_axis=0, concat_axis=0, tiled=True)


def on_device(queries, keys_pool, values_pool, rel_bias, out_grad, fetch_ids, slot_of):
    head = lax.axis_index("block").astype(jnp.int32).reshape(1)
    parts = pack_grads(head, out_grad)
    queries, *parts = lax.optimization_barrier((queries, *parts))
    parts = [parts[0]] + [send_by(parts[dx], dx, 0) for dx in range(1, X_SIZE)]
    sent = pack_queries(fetch_ids, slot_of, queries)
    recv = all_to_all(sent)
    grads = list(regroup(head, parts))
    recv, grads[0] = lax.optimization_barrier((recv, grads[0]))
    y = forward(head, recv, keys_pool, values_pool, rel_bias)
    y, grads[1], grads[7] = lax.optimization_barrier((y, grads[1], grads[7]))
    grads = [grads[0]] + [send_by(grads[dz], 0, dz) for dz in range(1, Z_SIZE)]
    back_y = all_to_all(y)
    recv, _ = lax.optimization_barrier((recv, y))
    dq, bias_part = query_grads(head, recv, grads, keys_pool, values_pool, rel_bias)
    dq = add_row(sum_groups(bias_part), dq)
    back_dq = all_to_all(dq)
    recv, _ = lax.optimization_barrier((recv, dq))
    key_grad, value_grad = pool_grads(head, recv, grads, keys_pool, values_pool, rel_bias)
    (attended,) = unpack(back_y)
    query_grad, bias_grad = unpack(back_dq)
    return (attended, query_grad, key_grad, value_grad, bias_grad)


def solution(mesh):
    in_specs = (
        P("dp", "block", None, None),
        P("dp", None, None, "block"),
        P("dp", None, None, "block"),
        P(),
        P("dp", "block", None, None),
        P("dp", "block", None),
        P("dp", "block", None),
    )
    out_specs = (
        P("dp", "block", None, None),
        P("dp", "block", None, None),
        P("dp", None, None, "block"),
        P("dp", None, None, "block"),
        P(),
    )
    return jax.shard_map(
        on_device, mesh=mesh, in_specs=in_specs, out_specs=out_specs, check_vma=False
    )
```

```python
import functools
import math

import jax
import jax.numpy as jnp
from jax import lax
from jax.experimental import pallas as pl
from jax.experimental.pallas import tpu as pltpu
from jax.sharding import PartitionSpec as P

HEADS = 32
HEAD_DIM = 128
BLOCK = 64
NBLEN = 128
NEIGH = 2
CH_DEV = 2
POOL = 32
HD = HEADS * HEAD_DIM
REL = 192
N_BLOCK = 32
N_DP = 8
X_SIZE = 4
Z_SIZE = 8
HALF = CH_DEV * BLOCK
EXTRA = 8
PACK_HEADS = 8
SCALE = 1.0 / math.sqrt(HEAD_DIM)

NT = (((1,), (1,)), ((), ()))
TN = (((0,), (0,)), ((), ()))
F32 = jnp.float32
BF16 = jnp.bfloat16


VMEM_SPEC = pl.BlockSpec(memory_space=pltpu.VMEM)
SMEM_SPEC = pl.BlockSpec(memory_space=pltpu.SMEM)
ANY_SPEC = pl.BlockSpec(memory_space=pl.ANY)
HBM_SPEC = pl.BlockSpec(memory_space=pltpu.HBM)
CHUNKS = HEADS // PACK_HEADS
CHUNK_WIDTH = PACK_HEADS * HEAD_DIM


def block_rows(c):
    return slice(c * BLOCK, (c + 1) * BLOCK)


def head_columns(h):
    return slice(h * HEAD_DIM, (h + 1) * HEAD_DIM)


def vmem_limit(mib):
    return pltpu.CompilerParams(vmem_limit_bytes=mib * 1024 * 1024)


def start(source, target, sem):
    copy = pltpu.make_async_copy(source, target, sem)
    copy.start()
    return copy


def pack_kernel(head_ref, fetch_ref, slot_ref, q_ref, g_ref, sent_ref, *refs):
    part_refs = refs[:X_SIZE]
    q_buf, g_buf, sent_buf, part_buf, q_sems, g_sems, sent_sems, part_sems = refs[X_SIZE:]
    g_copies, q_copies, outs = [], [], []
    for i in range(X_SIZE):
        column = lax.rem(head_ref[0] // Z_SIZE + i, X_SIZE) * CHUNK_WIDTH
        cols = pl.ds(pl.multiple_of(column, CHUNK_WIDTH), CHUNK_WIDTH)
        g_copies.append(start(g_ref.at[0, :, :, cols], g_buf.at[i], g_sems.at[i]))
    for i in range(CHUNKS):
        cols = slice(i * CHUNK_WIDTH, (i + 1) * CHUNK_WIDTH)
        q_copies.append(start(q_ref.at[0, :, :, cols], q_buf.at[:, :, cols], q_sems.at[i]))
    lane = lax.broadcasted_iota(jnp.int32, (EXTRA, 128), 1)
    ids = jnp.zeros((EXTRA, 128), jnp.int32)
    for c in range(CH_DEV):
        for n in range(NEIGH):
            enc = fetch_ref[0, 0, slot_ref[0, c, n]]
            ids = jnp.where(lane == c * NEIGH + n, enc, ids)
    ids = ids.astype(F32).astype(BF16)
    for i in range(X_SIZE):
        g_copies[i].wait()
        for h in range(Z_SIZE):
            for c in range(CH_DEV):
                part_buf[i, h, block_rows(c)] = g_buf[i, c, :, head_columns(h)]
        outs.append(start(part_buf.at[i], part_refs[i], part_sems.at[i]))
    for i in range(CHUNKS):
        heads = slice(i * PACK_HEADS, (i + 1) * PACK_HEADS)
        q_copies[i].wait()
        for h in range(i * PACK_HEADS, (i + 1) * PACK_HEADS):
            for c in range(CH_DEV):
                sent_buf[h, block_rows(c)] = q_buf[c, :, head_columns(h)]
            sent_buf[h, HALF:] = ids
        outs.append(start(sent_buf.at[heads], sent_ref.at[heads], sent_sems.at[i]))
    for copy in outs:
        copy.wait()


def pack(head, fetch_ids, slot_of, queries, out_grad):
    part = (Z_SIZE, HALF, HEAD_DIM)
    sent = (HEADS, HALF + EXTRA, HEAD_DIM)
    return pl.pallas_call(
        pack_kernel,
        in_specs=[SMEM_SPEC] * 3 + [ANY_SPEC] * 2,
        out_specs=[ANY_SPEC] * (1 + X_SIZE),
        out_shape=[jax.ShapeDtypeStruct(sent, BF16)] + [jax.ShapeDtypeStruct(part, BF16)] * X_SIZE,
        scratch_shapes=[
            pltpu.VMEM((CH_DEV, BLOCK, HD), BF16),
            pltpu.VMEM((X_SIZE, CH_DEV, BLOCK, CHUNK_WIDTH), BF16),
            pltpu.VMEM(sent, BF16),
            pltpu.VMEM((X_SIZE, *part), BF16),
            pltpu.SemaphoreType.DMA((CHUNKS,)),
            pltpu.SemaphoreType.DMA((X_SIZE,)),
            pltpu.SemaphoreType.DMA((CHUNKS,)),
            pltpu.SemaphoreType.DMA((X_SIZE,)),
        ],
        compiler_params=vmem_limit(60),
        cost_estimate=pl.CostEstimate(flops=10**11, bytes_accessed=4 * 10**6, transcendentals=0),
        name="pack_heads",
    )(head, fetch_ids, slot_of, queries, out_grad)


def regroup_kernel(head_ref, *refs):
    in_refs, out_refs = refs[:X_SIZE], refs[X_SIZE : X_SIZE + Z_SIZE]
    buf, in_sems, out_sems = refs[X_SIZE + Z_SIZE :]
    copies = [start(in_refs[i], buf.at[i], in_sems.at[i]) for i in range(X_SIZE)]
    for copy in copies:
        copy.wait()
    copies = []
    for k in range(Z_SIZE):
        owner = lax.rem(head_ref[0] + k, Z_SIZE)
        copies.append(start(buf.at[:, owner], out_refs[k], out_sems.at[k]))
    for copy in copies:
        copy.wait()


def regroup(head, parts):
    return pl.pallas_call(
        regroup_kernel,
        in_specs=[SMEM_SPEC] + [ANY_SPEC] * X_SIZE,
        out_specs=[ANY_SPEC] * Z_SIZE,
        out_shape=[jax.ShapeDtypeStruct((X_SIZE, HALF, HEAD_DIM), BF16)] * Z_SIZE,
        scratch_shapes=[
            pltpu.VMEM((X_SIZE, Z_SIZE, HALF, HEAD_DIM), BF16),
            pltpu.SemaphoreType.DMA((X_SIZE,)),
            pltpu.SemaphoreType.DMA((Z_SIZE,)),
        ],
        compiler_params=vmem_limit(60),
        cost_estimate=pl.CostEstimate(flops=10**11, bytes_accessed=2 * 10**6, transcendentals=0),
        name="regroup_grads",
    )(head, *parts)


def send_by(part, dx, dz):
    pairs = [
        (x * Z_SIZE + z, (x + dx) % X_SIZE * Z_SIZE + (z + dz) % Z_SIZE)
        for x in range(X_SIZE)
        for z in range(Z_SIZE)
    ]
    return lax.ppermute(part, "block", pairs)


def build_bias(rel_ref, head, bias_ref):
    row = rel_ref[pl.ds(head, 1), :]
    wide = jnp.concatenate([row, jnp.zeros((1, 256 - REL), F32)], axis=1)
    wide = jnp.broadcast_to(wide, (BLOCK, 256))
    rolled = pltpu.roll(wide, 256 - (BLOCK - 1), 1, stride=1, stride_axis=0)[:, :NBLEN]
    bias_ref[...] = jnp.concatenate([rolled, rolled], axis=1)


def fold_bias(dscore_sum):
    folded = dscore_sum[:, :NBLEN] + dscore_sum[:, NBLEN:]
    wide = jnp.concatenate([folded, jnp.zeros((BLOCK, NBLEN), F32)], axis=1)
    group = sum(
        pltpu.roll(wide[t : t + 8], BLOCK - 8 - t, 1) if t < BLOCK - 8 else wide[t : t + 8]
        for t in range(0, BLOCK, 8)
    )
    return sum(
        pltpu.roll(group[r : r + 1], 7 - r, 1) if r < 7 else group[r : r + 1] for r in range(8)
    )


def read_ids(x_ref, ids_vmem, ids_smem, sem):
    ids_vmem[...] = x_ref[:, HALF, :].astype(F32).astype(jnp.int32)
    copy = pltpu.make_async_copy(ids_vmem, ids_smem, sem)
    copy.start()
    return copy


WIDE = 2 * X_SIZE


def blocks_of(sources):
    return [(s, c) for s in range(len(sources)) for c in range(CH_DEV)]


def softmax_parts(sources, ids_smem, bias_ref, x_ref, keys_ref, values_ref):
    bias = bias_ref[...]
    blocks = blocks_of(sources)
    ids = [[ids_smem[sources[s], c * NEIGH + n] for n in range(NEIGH)] for s, c in blocks]
    q = [x_ref[sources[s], block_rows(c)] for s, c in blocks]
    k = [jnp.concatenate([keys_ref[0, i] for i in pair], axis=0) for pair in ids]
    v = [jnp.concatenate([values_ref[0, i] for i in pair], axis=0) for pair in ids]
    scores = [lax.dot_general(a, b, NT, preferred_element_type=F32) for a, b in zip(q, k)]
    scores = [a * SCALE + bias for a in scores]
    tops = [jnp.max(a, axis=-1, keepdims=True) for a in scores]
    expo = [jnp.exp(a - b) for a, b in zip(scores, tops)]
    inverse = [1.0 / jnp.sum(a, axis=-1, keepdims=True) for a in expo]
    probs = [a * b for a, b in zip(expo, inverse)]
    return ids, q, k, v, probs


def forward_kernel(
    head_ref, x_ref, keys_ref, values_ref, rel_ref, y_ref, ids_vmem, ids_smem, bias_ref, sem
):
    copy = read_ids(x_ref, ids_vmem, ids_smem, sem)
    build_bias(rel_ref, head_ref[0], bias_ref)
    copy.wait()

    def step(t, carry):
        sources = [t * WIDE + s for s in range(WIDE)]
        ids, q, k, v, probs = softmax_parts(
            sources, ids_smem, bias_ref, x_ref, keys_ref, values_ref
        )
        for i, (s, c) in enumerate(blocks_of(sources)):
            attended = jnp.dot(probs[i].astype(BF16), v[i], preferred_element_type=F32)
            y_ref[sources[s], block_rows(c)] = attended.astype(BF16)
        return carry

    lax.fori_loop(0, N_BLOCK // WIDE, step, 0)


def near_sources(index, t):
    x, z = index // Z_SIZE, lax.rem(index, Z_SIZE)
    z_source = lax.rem(z + Z_SIZE - t, Z_SIZE)
    return [lax.rem(x + X_SIZE - s, X_SIZE) * Z_SIZE + z_source for s in range(X_SIZE)]


def score_grads(index, times, ids_smem, bias_ref, x_ref, g_buf, keys_ref, values_ref):
    sources = [source for t in times for source in near_sources(index, t)]
    ids, q, k, v, probs = softmax_parts(
        sources, ids_smem, bias_ref, x_ref, keys_ref, values_ref
    )
    g = [g_buf[times[s // X_SIZE], s % X_SIZE, block_rows(c)] for s, c in blocks_of(sources)]
    dprobs = [lax.dot_general(a, b, NT, preferred_element_type=F32) for a, b in zip(g, v)]
    inner = [jnp.sum(a * b, axis=-1, keepdims=True) for a, b in zip(probs, dprobs)]
    dscores = [a * (b - c) for a, b, c in zip(probs, dprobs, inner)]
    return sources, ids, q, k, g, probs, dscores


def query_grad_kernel(head_ref, x_ref, keys_ref, values_ref, rel_ref, *refs):
    g_refs = refs[:Z_SIZE]
    y_ref, bias_out, ids_vmem, ids_smem, bias_ref, dsum_ref, g_buf, sem, g_sems = refs[Z_SIZE:]
    g_copies = [start(g_refs[k], g_buf.at[k], g_sems.at[k]) for k in range(Z_SIZE)]
    copy = read_ids(x_ref, ids_vmem, ids_smem, sem)
    build_bias(rel_ref, head_ref[0], bias_ref)
    dsum_ref[...] = jnp.zeros_like(dsum_ref)
    copy.wait()
    for g_copy in g_copies:
        g_copy.wait()

    def step(t, carry):
        sources, _, _, k, _, _, dscores = score_grads(
            head_ref[0], [2 * t, 2 * t + 1], ids_smem, bias_ref, x_ref, g_buf, keys_ref, values_ref
        )
        dsum_ref[...] += sum(dscores)
        for i, (s, c) in enumerate(blocks_of(sources)):
            low = dscores[i].astype(BF16)
            query_grad = jnp.dot(low, k[i], preferred_element_type=F32) * SCALE
            y_ref[sources[s], block_rows(c)] = query_grad.astype(BF16)
        return carry

    lax.fori_loop(0, Z_SIZE // 2, step, 0)
    bias_out[...] = fold_bias(dsum_ref[...])


def pool_grad_kernel(head_ref, x_ref, keys_ref, values_ref, rel_ref, *refs):
    g_refs = refs[:Z_SIZE]
    dk_out, dv_out, ids_vmem, ids_smem, bias_ref, dk_ref, dv_ref, g_buf, sem, g_sems = refs[Z_SIZE:]
    g_copies = [start(g_refs[k], g_buf.at[k], g_sems.at[k]) for k in range(Z_SIZE)]
    copy = read_ids(x_ref, ids_vmem, ids_smem, sem)
    build_bias(rel_ref, head_ref[0], bias_ref)
    dk_ref[...] = jnp.zeros_like(dk_ref)
    dv_ref[...] = jnp.zeros_like(dv_ref)
    copy.wait()
    for g_copy in g_copies:
        g_copy.wait()

    def step(t, carry):
        _, ids, q, _, g, probs, dscores = score_grads(
            head_ref[0], [t], ids_smem, bias_ref, x_ref, g_buf, keys_ref, values_ref
        )
        dscores_low = [a.astype(BF16) for a in dscores]
        probs_low = [a.astype(BF16) for a in probs]
        dk = [lax.dot_general(a, b, TN, preferred_element_type=F32) for a, b in zip(dscores_low, q)]
        dv = [lax.dot_general(a, b, TN, preferred_element_type=F32) for a, b in zip(probs_low, g)]
        for i in range(len(ids)):
            for n in range(NEIGH):
                rows = slice(n * NBLEN, (n + 1) * NBLEN)
                dk_ref[ids[i][n]] += dk[i][rows]
                dv_ref[ids[i][n]] += dv[i][rows]
        return carry

    lax.fori_loop(0, Z_SIZE, step, 0)
    dk_out[0] = (dk_ref[...] * SCALE).astype(BF16)
    dv_out[0] = dv_ref[...].astype(BF16)


POOL_SHAPE = (1, POOL, NBLEN, HEAD_DIM)
BIAS_SHAPE = (BLOCK, NEIGH * NBLEN)
IDS_SCRATCH = [pltpu.VMEM((N_BLOCK, 128), jnp.int32), pltpu.SMEM((N_BLOCK, 128), jnp.int32)]


def forward(head, recv, keys_pool, values_pool, rel_bias):
    return pl.pallas_call(
        forward_kernel,
        in_specs=[SMEM_SPEC] + [VMEM_SPEC] * 4,
        out_specs=VMEM_SPEC,
        out_shape=jax.ShapeDtypeStruct((N_BLOCK, HALF, HEAD_DIM), BF16),
        scratch_shapes=[*IDS_SCRATCH, pltpu.VMEM(BIAS_SHAPE, F32), pltpu.SemaphoreType.DMA],
        compiler_params=vmem_limit(16),
        cost_estimate=pl.CostEstimate(flops=10**11, bytes_accessed=4 * 10**6, transcendentals=10**6),
        name="attention_forward",
    )(head, recv, keys_pool, values_pool, rel_bias)


def query_grads(head, recv, grads, keys_pool, values_pool, rel_bias):
    return pl.pallas_call(
        query_grad_kernel,
        in_specs=[SMEM_SPEC] + [VMEM_SPEC] * 4 + [ANY_SPEC] * Z_SIZE,
        out_specs=[VMEM_SPEC] * 2,
        out_shape=[
            jax.ShapeDtypeStruct((N_BLOCK, HALF + EXTRA, HEAD_DIM), BF16),
            jax.ShapeDtypeStruct((1, 256), F32),
        ],
        scratch_shapes=[
            *IDS_SCRATCH,
            pltpu.VMEM(BIAS_SHAPE, F32),
            pltpu.VMEM(BIAS_SHAPE, F32),
            pltpu.VMEM((Z_SIZE, X_SIZE, HALF, HEAD_DIM), BF16),
            pltpu.SemaphoreType.DMA,
            pltpu.SemaphoreType.DMA((Z_SIZE,)),
        ],
        compiler_params=vmem_limit(16),
        cost_estimate=pl.CostEstimate(flops=10**11, bytes_accessed=5 * 10**6, transcendentals=10**6),
        name="query_grads",
    )(head, recv, keys_pool, values_pool, rel_bias, *grads)


def pool_grads(head, recv, grads, keys_pool, values_pool, rel_bias):
    return pl.pallas_call(
        pool_grad_kernel,
        in_specs=[SMEM_SPEC] + [VMEM_SPEC] * 4 + [ANY_SPEC] * Z_SIZE,
        out_specs=[VMEM_SPEC] * 2,
        out_shape=[jax.ShapeDtypeStruct(POOL_SHAPE, BF16)] * 2,
        scratch_shapes=[
            *IDS_SCRATCH,
            pltpu.VMEM(BIAS_SHAPE, F32),
            pltpu.VMEM(POOL_SHAPE[1:], F32),
            pltpu.VMEM(POOL_SHAPE[1:], F32),
            pltpu.VMEM((Z_SIZE, X_SIZE, HALF, HEAD_DIM), BF16),
            pltpu.SemaphoreType.DMA,
            pltpu.SemaphoreType.DMA((Z_SIZE,)),
        ],
        compiler_params=vmem_limit(24),
        cost_estimate=pl.CostEstimate(flops=10**11, bytes_accessed=6 * 10**6, transcendentals=10**6),
        name="pool_grads",
    )(head, recv, keys_pool, values_pool, rel_bias, *grads)


def add_row_kernel(row_ref, _, y_ref, block_ref, sem):
    row = row_ref[...]
    high = row.astype(BF16)
    rest = row - high.astype(F32)
    middle = rest.astype(BF16)
    low = (rest - middle.astype(F32)).astype(BF16)
    lines = [part.astype(F32)[:, c : c + 128] for part in (high, middle, low) for c in (0, 128)]
    block = jnp.concatenate([*lines, jnp.zeros((EXTRA - 6, 128), F32)], axis=0).astype(BF16)
    block_ref[...] = jnp.broadcast_to(block[None], block_ref.shape)
    copy = pltpu.make_async_copy(block_ref, y_ref.at[:, HALF:], sem)
    copy.start()
    copy.wait()


def add_row(row, y):
    return pl.pallas_call(
        add_row_kernel,
        in_specs=[VMEM_SPEC, ANY_SPEC],
        out_specs=ANY_SPEC,
        out_shape=jax.ShapeDtypeStruct(y.shape, BF16),
        scratch_shapes=[pltpu.VMEM((N_BLOCK, EXTRA, HEAD_DIM), BF16), pltpu.SemaphoreType.DMA],
        input_output_aliases={1: 0},
        compiler_params=vmem_limit(4),
        name="add_bias_row",
    )(row, y)


def unpack_kernel(y_ref, out_ref, buf, sems):
    copies = []
    for i in range(CHUNKS):
        for h in range(i * PACK_HEADS, (i + 1) * PACK_HEADS):
            for c in range(CH_DEV):
                buf[c, :, head_columns(h)] = y_ref[h, block_rows(c)]
        cols = slice(i * CHUNK_WIDTH, (i + 1) * CHUNK_WIDTH)
        copy = pltpu.make_async_copy(buf.at[:, :, cols], out_ref.at[0, :, :, cols], sems.at[i])
        copy.start()
        copies.append(copy)
    for copy in copies:
        copy.wait()


def unpack_bias_kernel(y_ref, out_ref, bias_ref, buf, sems):
    lines = y_ref[:, HALF:, :].astype(F32)
    part = [lines[:, r, :] for r in range(6)]
    left = (part[0] + part[2]) + part[4]
    right = (part[1] + part[3]) + part[5]
    bias_ref[...] = jnp.concatenate([left, right], axis=1)[:, :REL]
    unpack_kernel(y_ref, out_ref, buf, sems)


def unpack(back):
    shape = jax.ShapeDtypeStruct((1, CH_DEV, BLOCK, HD), BF16)
    with_bias = back.shape[1] > HALF
    return pl.pallas_call(
        unpack_bias_kernel if with_bias else unpack_kernel,
        in_specs=[VMEM_SPEC],
        out_specs=[HBM_SPEC] + [VMEM_SPEC] * with_bias,
        out_shape=[shape] + [jax.ShapeDtypeStruct((HEADS, REL), F32)] * with_bias,
        scratch_shapes=[pltpu.VMEM((CH_DEV, BLOCK, HD), BF16), pltpu.SemaphoreType.DMA((CHUNKS,))],
        compiler_params=vmem_limit(8),
        name="unpack_heads",
    )(back)


def sum_groups(part):
    def swap(value, hop):
        return lax.ppermute(value, "dp", [(d, d ^ hop) for d in range(N_DP)])

    part = part + swap(part, 1)
    other, third, fourth = swap(part, 2), swap(part, 4), swap(part, 6)
    return (part + other) + (third + fourth)


def all_to_all(parts):
    return lax.all_to_all(parts, "block", split_axis=0, concat_axis=0, tiled=True)


def on_device(queries, keys_pool, values_pool, rel_bias, out_grad, fetch_ids, slot_of):
    head = lax.axis_index("block").astype(jnp.int32).reshape(1)
    sent, *parts = pack(head, fetch_ids, slot_of, queries, out_grad)
    parts = [parts[0]] + [send_by(parts[dx], dx, 0) for dx in range(1, X_SIZE)]
    recv = all_to_all(sent)
    grads = list(regroup(head, parts))
    recv, grads[0] = lax.optimization_barrier((recv, grads[0]))
    y = forward(head, recv, keys_pool, values_pool, rel_bias)
    y, grads[3], grads[5] = lax.optimization_barrier((y, grads[3], grads[5]))
    grads = [grads[0]] + [send_by(grads[dz], 0, dz) for dz in range(1, Z_SIZE)]
    back_y = all_to_all(y)
    recv, _ = lax.optimization_barrier((recv, y))
    dq, bias_part = query_grads(head, recv, grads, keys_pool, values_pool, rel_bias)
    dq = add_row(sum_groups(bias_part), dq)
    back_dq = all_to_all(dq)
    recv, _ = lax.optimization_barrier((recv, dq))
    key_grad, value_grad = pool_grads(head, recv, grads, keys_pool, values_pool, rel_bias)
    (attended,) = unpack(back_y)
    query_grad, bias_grad = unpack(back_dq)
    return (attended, query_grad, key_grad, value_grad, bias_grad)


def solution(mesh):
    in_specs = (
        P("dp", "block", None, None),
        P("dp", None, None, "block"),
        P("dp", None, None, "block"),
        P(),
        P("dp", "block", None, None),
        P("dp", "block", None),
        P("dp", "block", None),
    )
    out_specs = (
        P("dp", "block", None, None),
        P("dp", "block", None, None),
        P("dp", None, None, "block"),
        P("dp", None, None, "block"),
        P(),
    )
    return jax.shard_map(
        on_device, mesh=mesh, in_specs=in_specs, out_specs=out_specs, check_vma=False
    )
```

```python
import functools
import math

import jax
import jax.numpy as jnp
from jax import lax
from jax.experimental import pallas as pl
from jax.experimental.pallas import tpu as pltpu
from jax.sharding import PartitionSpec as P

HEADS = 32
HEAD_DIM = 128
BLOCK = 64
NBLEN = 128
NEIGH = 2
CH_DEV = 2
POOL = 32
HD = HEADS * HEAD_DIM
REL = 192
N_BLOCK = 32
N_DP = 8
X_SIZE = 4
Z_SIZE = 8
HALF = CH_DEV * BLOCK
EXTRA = 8
PACK_HEADS = 8
SCALE = 1.0 / math.sqrt(HEAD_DIM)

NT = (((1,), (1,)), ((), ()))
TN = (((0,), (0,)), ((), ()))
F32 = jnp.float32
BF16 = jnp.bfloat16


VMEM_SPEC = pl.BlockSpec(memory_space=pltpu.VMEM)
SMEM_SPEC = pl.BlockSpec(memory_space=pltpu.SMEM)
ANY_SPEC = pl.BlockSpec(memory_space=pl.ANY)
HBM_SPEC = pl.BlockSpec(memory_space=pltpu.HBM)
CHUNKS = HEADS // PACK_HEADS
CHUNK_WIDTH = PACK_HEADS * HEAD_DIM


def block_rows(c):
    return slice(c * BLOCK, (c + 1) * BLOCK)


def head_columns(h):
    return slice(h * HEAD_DIM, (h + 1) * HEAD_DIM)


def vmem_limit(mib):
    return pltpu.CompilerParams(vmem_limit_bytes=mib * 1024 * 1024)


def start(source, target, sem):
    copy = pltpu.make_async_copy(source, target, sem)
    copy.start()
    return copy


def pack_kernel(head_ref, fetch_ref, slot_ref, q_ref, g_ref, sent_ref, *refs):
    part_refs = refs[:X_SIZE]
    q_buf, g_buf, sent_buf, part_buf, q_sems, g_sems, sent_sems, part_sems = refs[X_SIZE:]
    g_copies, q_copies, outs = [], [], []
    for i in range(X_SIZE):
        column = lax.rem(head_ref[0] // Z_SIZE + i, X_SIZE) * CHUNK_WIDTH
        cols = pl.ds(pl.multiple_of(column, CHUNK_WIDTH), CHUNK_WIDTH)
        g_copies.append(start(g_ref.at[0, :, :, cols], g_buf.at[i], g_sems.at[i]))
    for i in range(CHUNKS):
        cols = slice(i * CHUNK_WIDTH, (i + 1) * CHUNK_WIDTH)
        q_copies.append(start(q_ref.at[0, :, :, cols], q_buf.at[:, :, cols], q_sems.at[i]))
    lane = lax.broadcasted_iota(jnp.int32, (EXTRA, 128), 1)
    ids = jnp.zeros((EXTRA, 128), jnp.int32)
    for c in range(CH_DEV):
        for n in range(NEIGH):
            enc = fetch_ref[0, 0, slot_ref[0, c, n]]
            ids = jnp.where(lane == c * NEIGH + n, enc, ids)
    ids = ids.astype(F32).astype(BF16)
    for i in range(X_SIZE):
        g_copies[i].wait()
        for h in range(Z_SIZE):
            for c in range(CH_DEV):
                part_buf[i, h, block_rows(c)] = g_buf[i, c, :, head_columns(h)]
        outs.append(start(part_buf.at[i], part_refs[i], part_sems.at[i]))
    for i in range(CHUNKS):
        heads = slice(i * PACK_HEADS, (i + 1) * PACK_HEADS)
        q_copies[i].wait()
        for h in range(i * PACK_HEADS, (i + 1) * PACK_HEADS):
            for c in range(CH_DEV):
                sent_buf[h, block_rows(c)] = q_buf[c, :, head_columns(h)]
            sent_buf[h, HALF:] = ids
        outs.append(start(sent_buf.at[heads], sent_ref.at[heads], sent_sems.at[i]))
    for copy in outs:
        copy.wait()


def pack(head, fetch_ids, slot_of, queries, out_grad):
    part = (Z_SIZE, HALF, HEAD_DIM)
    sent = (HEADS, HALF + EXTRA, HEAD_DIM)
    return pl.pallas_call(
        pack_kernel,
        in_specs=[SMEM_SPEC] * 3 + [ANY_SPEC] * 2,
        out_specs=[ANY_SPEC] * (1 + X_SIZE),
        out_shape=[jax.ShapeDtypeStruct(sent, BF16)] + [jax.ShapeDtypeStruct(part, BF16)] * X_SIZE,
        scratch_shapes=[
            pltpu.VMEM((CH_DEV, BLOCK, HD), BF16),
            pltpu.VMEM((X_SIZE, CH_DEV, BLOCK, CHUNK_WIDTH), BF16),
            pltpu.VMEM(sent, BF16),
            pltpu.VMEM((X_SIZE, *part), BF16),
            pltpu.SemaphoreType.DMA((CHUNKS,)),
            pltpu.SemaphoreType.DMA((X_SIZE,)),
            pltpu.SemaphoreType.DMA((CHUNKS,)),
            pltpu.SemaphoreType.DMA((X_SIZE,)),
        ],
        compiler_params=vmem_limit(60),
        cost_estimate=pl.CostEstimate(flops=10**11, bytes_accessed=4 * 10**6, transcendentals=0),
        name="pack_heads",
    )(head, fetch_ids, slot_of, queries, out_grad)


def regroup_kernel(head_ref, *refs):
    in_refs, out_refs = refs[:X_SIZE], refs[X_SIZE : X_SIZE + Z_SIZE]
    buf, in_sems, out_sems = refs[X_SIZE + Z_SIZE :]
    copies = [start(in_refs[i], buf.at[i], in_sems.at[i]) for i in range(X_SIZE)]
    for copy in copies:
        copy.wait()
    copies = []
    for k in range(Z_SIZE):
        owner = lax.rem(head_ref[0] + k, Z_SIZE)
        copies.append(start(buf.at[:, owner], out_refs[k], out_sems.at[k]))
    for copy in copies:
        copy.wait()


def regroup(head, parts):
    return pl.pallas_call(
        regroup_kernel,
        in_specs=[SMEM_SPEC] + [ANY_SPEC] * X_SIZE,
        out_specs=[ANY_SPEC] * Z_SIZE,
        out_shape=[jax.ShapeDtypeStruct((X_SIZE, HALF, HEAD_DIM), BF16)] * Z_SIZE,
        scratch_shapes=[
            pltpu.VMEM((X_SIZE, Z_SIZE, HALF, HEAD_DIM), BF16),
            pltpu.SemaphoreType.DMA((X_SIZE,)),
            pltpu.SemaphoreType.DMA((Z_SIZE,)),
        ],
        compiler_params=vmem_limit(60),
        cost_estimate=pl.CostEstimate(flops=10**11, bytes_accessed=2 * 10**6, transcendentals=0),
        name="regroup_grads",
    )(head, *parts)


def send_by(part, dx, dz):
    pairs = [
        (x * Z_SIZE + z, (x + dx) % X_SIZE * Z_SIZE + (z + dz) % Z_SIZE)
        for x in range(X_SIZE)
        for z in range(Z_SIZE)
    ]
    return lax.ppermute(part, "block", pairs)


def build_bias(rel_ref, head, bias_ref):
    row = rel_ref[pl.ds(head, 1), :]
    wide = jnp.concatenate([row, jnp.zeros((1, 256 - REL), F32)], axis=1)
    wide = jnp.broadcast_to(wide, (BLOCK, 256))
    rolled = pltpu.roll(wide, 256 - (BLOCK - 1), 1, stride=1, stride_axis=0)[:, :NBLEN]
    bias_ref[...] = jnp.concatenate([rolled, rolled], axis=1)


def fold_bias(dscore_sum):
    folded = dscore_sum[:, :NBLEN] + dscore_sum[:, NBLEN:]
    wide = jnp.concatenate([folded, jnp.zeros((BLOCK, NBLEN), F32)], axis=1)
    group = sum(
        pltpu.roll(wide[t : t + 8], BLOCK - 8 - t, 1) if t < BLOCK - 8 else wide[t : t + 8]
        for t in range(0, BLOCK, 8)
    )
    return sum(
        pltpu.roll(group[r : r + 1], 7 - r, 1) if r < 7 else group[r : r + 1] for r in range(8)
    )


def read_ids(x_ref, ids_vmem, ids_smem, sem):
    ids_vmem[...] = x_ref[:, HALF, :].astype(F32).astype(jnp.int32)
    copy = pltpu.make_async_copy(ids_vmem, ids_smem, sem)
    copy.start()
    return copy


WIDE = 2 * X_SIZE


def blocks_of(sources):
    return [(s, c) for s in range(len(sources)) for c in range(CH_DEV)]


def softmax_parts(sources, ids_smem, bias_ref, x_ref, keys_ref, values_ref):
    bias = bias_ref[...]
    blocks = blocks_of(sources)
    ids = [[ids_smem[sources[s], c * NEIGH + n] for n in range(NEIGH)] for s, c in blocks]
    q = [x_ref[sources[s], block_rows(c)] for s, c in blocks]
    k = [jnp.concatenate([keys_ref[0, i] for i in pair], axis=0) for pair in ids]
    v = [jnp.concatenate([values_ref[0, i] for i in pair], axis=0) for pair in ids]
    scores = [lax.dot_general(a, b, NT, preferred_element_type=F32) for a, b in zip(q, k)]
    scores = [a * SCALE + bias for a in scores]
    tops = [jnp.max(a, axis=-1, keepdims=True) for a in scores]
    expo = [jnp.exp(a - b) for a, b in zip(scores, tops)]
    inverse = [1.0 / jnp.sum(a, axis=-1, keepdims=True) for a in expo]
    probs = [a * b for a, b in zip(expo, inverse)]
    return ids, q, k, v, probs


def forward_kernel(
    head_ref, x_ref, keys_ref, values_ref, rel_ref, y_ref, ids_vmem, ids_smem, bias_ref, sem
):
    copy = read_ids(x_ref, ids_vmem, ids_smem, sem)
    build_bias(rel_ref, head_ref[0], bias_ref)
    copy.wait()

    def step(t, carry):
        sources = [t * WIDE + s for s in range(WIDE)]
        ids, q, k, v, probs = softmax_parts(
            sources, ids_smem, bias_ref, x_ref, keys_ref, values_ref
        )
        for i, (s, c) in enumerate(blocks_of(sources)):
            attended = jnp.dot(probs[i].astype(BF16), v[i], preferred_element_type=F32)
            y_ref[sources[s], block_rows(c)] = attended.astype(BF16)
        return carry

    lax.fori_loop(0, N_BLOCK // WIDE, step, 0)


def near_sources(index, t):
    x, z = index // Z_SIZE, lax.rem(index, Z_SIZE)
    z_source = lax.rem(z + Z_SIZE - t, Z_SIZE)
    return [lax.rem(x + X_SIZE - s, X_SIZE) * Z_SIZE + z_source for s in range(X_SIZE)]


def score_grads(index, times, ids_smem, bias_ref, x_ref, g_buf, keys_ref, values_ref):
    sources = [source for t in times for source in near_sources(index, t)]
    ids, q, k, v, probs = softmax_parts(
        sources, ids_smem, bias_ref, x_ref, keys_ref, values_ref
    )
    g = [g_buf[times[s // X_SIZE], s % X_SIZE, block_rows(c)] for s, c in blocks_of(sources)]
    dprobs = [lax.dot_general(a, b, NT, preferred_element_type=F32) for a, b in zip(g, v)]
    inner = [jnp.sum(a * b, axis=-1, keepdims=True) for a, b in zip(probs, dprobs)]
    dscores = [a * (b - c) for a, b, c in zip(probs, dprobs, inner)]
    return sources, ids, q, k, g, probs, dscores


def query_grad_kernel(head_ref, x_ref, keys_ref, values_ref, rel_ref, *refs):
    g_refs = refs[:Z_SIZE]
    y_ref, bias_out, ids_vmem, ids_smem, bias_ref, dsum_ref, g_buf, sem, g_sems = refs[Z_SIZE:]
    g_copies = [start(g_refs[k], g_buf.at[k], g_sems.at[k]) for k in range(Z_SIZE)]
    copy = read_ids(x_ref, ids_vmem, ids_smem, sem)
    build_bias(rel_ref, head_ref[0], bias_ref)
    dsum_ref[...] = jnp.zeros_like(dsum_ref)
    copy.wait()
    for g_copy in g_copies:
        g_copy.wait()

    def step(t, carry):
        sources, _, _, k, _, _, dscores = score_grads(
            head_ref[0], [4 * t + u for u in range(4)], ids_smem, bias_ref, x_ref, g_buf, keys_ref, values_ref
        )
        dsum_ref[...] += sum(dscores)
        for i, (s, c) in enumerate(blocks_of(sources)):
            low = dscores[i].astype(BF16)
            query_grad = jnp.dot(low, k[i], preferred_element_type=F32) * SCALE
            y_ref[sources[s], block_rows(c)] = query_grad.astype(BF16)
        return carry

    lax.fori_loop(0, Z_SIZE // 4, step, 0)
    bias_out[...] = fold_bias(dsum_ref[...])


def pool_grad_kernel(head_ref, x_ref, keys_ref, values_ref, rel_ref, *refs):
    g_refs = refs[:Z_SIZE]
    dk_out, dv_out, ids_vmem, ids_smem, bias_ref, dk_ref, dv_ref, g_buf, sem, g_sems = refs[Z_SIZE:]
    g_copies = [start(g_refs[k], g_buf.at[k], g_sems.at[k]) for k in range(Z_SIZE)]
    copy = read_ids(x_ref, ids_vmem, ids_smem, sem)
    build_bias(rel_ref, head_ref[0], bias_ref)
    dk_ref[...] = jnp.zeros_like(dk_ref)
    dv_ref[...] = jnp.zeros_like(dv_ref)
    copy.wait()
    for g_copy in g_copies:
        g_copy.wait()

    def step(t, carry):
        _, ids, q, _, g, probs, dscores = score_grads(
            head_ref[0], [t], ids_smem, bias_ref, x_ref, g_buf, keys_ref, values_ref
        )
        dscores_low = [a.astype(BF16) for a in dscores]
        probs_low = [a.astype(BF16) for a in probs]
        dk = [lax.dot_general(a, b, TN, preferred_element_type=F32) for a, b in zip(dscores_low, q)]
        dv = [lax.dot_general(a, b, TN, preferred_element_type=F32) for a, b in zip(probs_low, g)]
        for i in range(len(ids)):
            for n in range(NEIGH):
                rows = slice(n * NBLEN, (n + 1) * NBLEN)
                dk_ref[ids[i][n]] += dk[i][rows]
                dv_ref[ids[i][n]] += dv[i][rows]
        return carry

    lax.fori_loop(0, Z_SIZE, step, 0)
    dk_out[0] = (dk_ref[...] * SCALE).astype(BF16)
    dv_out[0] = dv_ref[...].astype(BF16)


POOL_SHAPE = (1, POOL, NBLEN, HEAD_DIM)
BIAS_SHAPE = (BLOCK, NEIGH * NBLEN)
IDS_SCRATCH = [pltpu.VMEM((N_BLOCK, 128), jnp.int32), pltpu.SMEM((N_BLOCK, 128), jnp.int32)]


def forward(head, recv, keys_pool, values_pool, rel_bias):
    return pl.pallas_call(
        forward_kernel,
        in_specs=[SMEM_SPEC] + [VMEM_SPEC] * 4,
        out_specs=VMEM_SPEC,
        out_shape=jax.ShapeDtypeStruct((N_BLOCK, HALF, HEAD_DIM), BF16),
        scratch_shapes=[*IDS_SCRATCH, pltpu.VMEM(BIAS_SHAPE, F32), pltpu.SemaphoreType.DMA],
        compiler_params=vmem_limit(16),
        cost_estimate=pl.CostEstimate(flops=10**11, bytes_accessed=4 * 10**6, transcendentals=10**6),
        name="attention_forward",
    )(head, recv, keys_pool, values_pool, rel_bias)


def query_grads(head, recv, grads, keys_pool, values_pool, rel_bias):
    return pl.pallas_call(
        query_grad_kernel,
        in_specs=[SMEM_SPEC] + [VMEM_SPEC] * 4 + [ANY_SPEC] * Z_SIZE,
        out_specs=[VMEM_SPEC] * 2,
        out_shape=[
            jax.ShapeDtypeStruct((N_BLOCK, HALF + EXTRA, HEAD_DIM), BF16),
            jax.ShapeDtypeStruct((1, 256), F32),
        ],
        scratch_shapes=[
            *IDS_SCRATCH,
            pltpu.VMEM(BIAS_SHAPE, F32),
            pltpu.VMEM(BIAS_SHAPE, F32),
            pltpu.VMEM((Z_SIZE, X_SIZE, HALF, HEAD_DIM), BF16),
            pltpu.SemaphoreType.DMA,
            pltpu.SemaphoreType.DMA((Z_SIZE,)),
        ],
        compiler_params=vmem_limit(16),
        cost_estimate=pl.CostEstimate(flops=10**11, bytes_accessed=5 * 10**6, transcendentals=10**6),
        name="query_grads",
    )(head, recv, keys_pool, values_pool, rel_bias, *grads)


def pool_grads(head, recv, grads, keys_pool, values_pool, rel_bias):
    return pl.pallas_call(
        pool_grad_kernel,
        in_specs=[SMEM_SPEC] + [VMEM_SPEC] * 4 + [ANY_SPEC] * Z_SIZE,
        out_specs=[VMEM_SPEC] * 2,
        out_shape=[jax.ShapeDtypeStruct(POOL_SHAPE, BF16)] * 2,
        scratch_shapes=[
            *IDS_SCRATCH,
            pltpu.VMEM(BIAS_SHAPE, F32),
            pltpu.VMEM(POOL_SHAPE[1:], F32),
            pltpu.VMEM(POOL_SHAPE[1:], F32),
            pltpu.VMEM((Z_SIZE, X_SIZE, HALF, HEAD_DIM), BF16),
            pltpu.SemaphoreType.DMA,
            pltpu.SemaphoreType.DMA((Z_SIZE,)),
        ],
        compiler_params=vmem_limit(24),
        cost_estimate=pl.CostEstimate(flops=10**11, bytes_accessed=6 * 10**6, transcendentals=10**6),
        name="pool_grads",
    )(head, recv, keys_pool, values_pool, rel_bias, *grads)


def add_row_kernel(row_ref, _, y_ref, block_ref, sem):
    row = row_ref[...]
    high = row.astype(BF16)
    rest = row - high.astype(F32)
    middle = rest.astype(BF16)
    low = (rest - middle.astype(F32)).astype(BF16)
    lines = [part.astype(F32)[:, c : c + 128] for part in (high, middle, low) for c in (0, 128)]
    block = jnp.concatenate([*lines, jnp.zeros((EXTRA - 6, 128), F32)], axis=0).astype(BF16)
    block_ref[...] = jnp.broadcast_to(block[None], block_ref.shape)
    copy = pltpu.make_async_copy(block_ref, y_ref.at[:, HALF:], sem)
    copy.start()
    copy.wait()


def add_row(row, y):
    return pl.pallas_call(
        add_row_kernel,
        in_specs=[VMEM_SPEC, ANY_SPEC],
        out_specs=ANY_SPEC,
        out_shape=jax.ShapeDtypeStruct(y.shape, BF16),
        scratch_shapes=[pltpu.VMEM((N_BLOCK, EXTRA, HEAD_DIM), BF16), pltpu.SemaphoreType.DMA],
        input_output_aliases={1: 0},
        compiler_params=vmem_limit(4),
        name="add_bias_row",
    )(row, y)


def unpack_kernel(y_ref, out_ref, buf, sems):
    copies = []
    for i in range(CHUNKS):
        for h in range(i * PACK_HEADS, (i + 1) * PACK_HEADS):
            for c in range(CH_DEV):
                buf[c, :, head_columns(h)] = y_ref[h, block_rows(c)]
        cols = slice(i * CHUNK_WIDTH, (i + 1) * CHUNK_WIDTH)
        copy = pltpu.make_async_copy(buf.at[:, :, cols], out_ref.at[0, :, :, cols], sems.at[i])
        copy.start()
        copies.append(copy)
    for copy in copies:
        copy.wait()


def unpack_bias_kernel(y_ref, out_ref, bias_ref, buf, sems):
    lines = y_ref[:, HALF:, :].astype(F32)
    part = [lines[:, r, :] for r in range(6)]
    left = (part[0] + part[2]) + part[4]
    right = (part[1] + part[3]) + part[5]
    bias_ref[...] = jnp.concatenate([left, right], axis=1)[:, :REL]
    unpack_kernel(y_ref, out_ref, buf, sems)


def unpack(back):
    shape = jax.ShapeDtypeStruct((1, CH_DEV, BLOCK, HD), BF16)
    with_bias = back.shape[1] > HALF
    return pl.pallas_call(
        unpack_bias_kernel if with_bias else unpack_kernel,
        in_specs=[VMEM_SPEC],
        out_specs=[HBM_SPEC] + [VMEM_SPEC] * with_bias,
        out_shape=[shape] + [jax.ShapeDtypeStruct((HEADS, REL), F32)] * with_bias,
        scratch_shapes=[pltpu.VMEM((CH_DEV, BLOCK, HD), BF16), pltpu.SemaphoreType.DMA((CHUNKS,))],
        compiler_params=vmem_limit(8),
        name="unpack_heads",
    )(back)


def sum_groups(part):
    def swap(value, hop):
        return lax.ppermute(value, "dp", [(d, d ^ hop) for d in range(N_DP)])

    part = part + swap(part, 1)
    other, third, fourth = swap(part, 2), swap(part, 4), swap(part, 6)
    return (part + other) + (third + fourth)


def all_to_all(parts):
    return lax.all_to_all(parts, "block", split_axis=0, concat_axis=0, tiled=True)


def on_device(queries, keys_pool, values_pool, rel_bias, out_grad, fetch_ids, slot_of):
    head = lax.axis_index("block").astype(jnp.int32).reshape(1)
    sent, *parts = pack(head, fetch_ids, slot_of, queries, out_grad)
    parts = [parts[0]] + [send_by(parts[dx], dx, 0) for dx in range(1, X_SIZE)]
    recv = all_to_all(sent)
    grads = list(regroup(head, parts))
    recv, grads[0] = lax.optimization_barrier((recv, grads[0]))
    y = forward(head, recv, keys_pool, values_pool, rel_bias)
    y, grads[3], grads[5] = lax.optimization_barrier((y, grads[3], grads[5]))
    grads = [grads[0]] + [send_by(grads[dz], 0, dz) for dz in range(1, Z_SIZE)]
    back_y = all_to_all(y)
    recv, _ = lax.optimization_barrier((recv, y))
    dq, bias_part = query_grads(head, recv, grads, keys_pool, values_pool, rel_bias)
    dq = add_row(sum_groups(bias_part), dq)
    back_dq = all_to_all(dq)
    recv, _ = lax.optimization_barrier((recv, dq))
    key_grad, value_grad = pool_grads(head, recv, grads, keys_pool, values_pool, rel_bias)
    (attended,) = unpack(back_y)
    query_grad, bias_grad = unpack(back_dq)
    return (attended, query_grad, key_grad, value_grad, bias_grad)


def solution(mesh):
    in_specs = (
        P("dp", "block", None, None),
        P("dp", None, None, "block"),
        P("dp", None, None, "block"),
        P(),
        P("dp", "block", None, None),
        P("dp", "block", None),
        P("dp", "block", None),
    )
    out_specs = (
        P("dp", "block", None, None),
        P("dp", "block", None, None),
        P("dp", None, None, "block"),
        P("dp", None, None, "block"),
        P(),
    )
    return jax.shard_map(
        on_device, mesh=mesh, in_specs=in_specs, out_specs=out_specs, check_vma=False
    )
```
